128 devices in a mesh: dp: 64 (over x, y, z), cores: 2 (over core).
Axes of the slice: x: 4, y: 4, z: 4, core: 2. Of those that a mesh axis runs over, the one named last changes fastest.
Arguments:
- queries: bfloat16 [65536, 1024], P(('dp', 'cores')), may hold values from -4 to 4
- passages: bfloat16 [65536, 1024], P(('dp', 'cores')), may hold values from -4 to 4
- positives: int32 [128, 512], P(('dp', 'cores')), may hold values from 0 to 511, each once within a row
- pair_blocks: int32 [128, 8], P(('dp', 'cores')), may hold values from 0 to 127, as said below
- negative_pair_count: int32 [128], P(('dp', 'cores')), may hold values from 1 to 8, as said below
Outputs:
- query_loss: float32 [128, 512], P(('dp', 'cores'))
- passage_loss: float32 [128, 512], P(('dp', 'cores'))
- query_grad: float32 [65536, 1024], P(('dp', 'cores'))
- passage_grad: float32 [65536, 1024], P(('dp', 'cores'))
The draws below stay inside these ranges and needn't reach their ends.
Inputs may be any that keep to these rules, and one draw needn't show every extreme that they name: `pair_blocks`: row b lists 8 different blocks, each (b + o) mod 128 with 1 <= |o| <= 4, so every block within 4 of b in cyclic order appears once. `negative_pair_count`: some block has 8 hard negatives and some block has 1 in every draw.
All inputs are finite; a program needn't handle non-finite values.
Results may differ from the reference program's by a relative error of at most 0.0022.
Values may be sent and summed in bfloat16 or wider, within the bound.
No kernel may reach another device: no remote copies, remote signals or barrier semaphores. Data moves between devices by JAX's collectives and lax.ppermute only.
A program may use at most 128 MiB of HBM per device.

```python
import math
import jax
import jax.numpy as jnp
from jax import lax

D = 1024
BLK = 512
RANGE = 4
NEG = 8
NB = 128
ROWS = 65536


def newly_arrived_entries(key, low, high):
    scale = jnp.exp(jax.random.uniform(jax.random.fold_in(key, 2), (ROWS, 1), jnp.float32, math.log(low), math.log(high)))
    values = jax.random.truncated_normal(key, -5.0, 5.0, (ROWS, D), jnp.float32)
    return scale * values / math.sqrt(D)


def embeddings(key, constant):
    key = jax.random.fold_in(key, constant)
    values = newly_arrived_entries(key, 0.5, 2.5)
    return values.astype(jnp.bfloat16)


def draw_queries(key, part):
    return embeddings(key, 11)


def draw_passages(key, part):
    return embeddings(key, 17)


def draw_pair_blocks(key, part):
    key = jax.random.fold_in(key, 31)
    keys = jax.random.split(key, NB)
    offsets = jnp.concatenate([jnp.arange(-RANGE, 0), jnp.arange(1, RANGE + 1)]).astype(jnp.int32)
    order = jax.vmap(lambda lone_example: jax.random.permutation(lone_example, offsets))(keys)
    return ((jnp.arange(NB, dtype=jnp.int32)[:, None] + order) % NB).astype(jnp.int32)


def draw_negative_pair_count(key, part):
    key = jax.random.fold_in(key, 41)
    count = jax.random.randint(key, (NB,), 1, NEG + 1).astype(jnp.int32)
    chosen_passage = jax.random.randint(jax.random.fold_in(key, 1), (), 0, NB)
    count = count.at[chosen_passage].set(NEG)
    count = count.at[(chosen_passage + 1) % NB].set(1)
    return count.astype(jnp.int32)


def setup_inputs(seed: int = 0) -> dict:
    seeds = jax.random.split(jax.random.key(seed), 6)
    queries = draw_queries(jax.random.fold_in(seeds[5], 71), 0)
    passages = draw_passages(jax.random.fold_in(seeds[5], 71), 0)
    positives = jax.vmap(lambda own: jax.random.permutation(own, BLK))(jax.random.split(seeds[2], NB)).reshape((NB, BLK)).astype(jnp.int32)
    pair_blocks = draw_pair_blocks(jax.random.fold_in(seeds[5], 71), 0)
    negative_pair_count = draw_negative_pair_count(jax.random.fold_in(seeds[5], 71), 0)
    return dict(queries=queries, passages=passages, positives=positives, pair_blocks=pair_blocks, negative_pair_count=negative_pair_count)


logit_multiplier = 20.0
far_negative = -1.0e30


def slot_offsets(reach):
    return [0] + [offset for offset in range(-reach, reach + 1) if offset != 0]


def slot_mask(pair_blocks, negative_pair_count, block_ids, blocks, reach):
    listed = pair_blocks.shape[1]
    used = jnp.arange(listed, dtype=jnp.int32)[None, :] < negative_pair_count[:, None]
    columns = []
    for offset in slot_offsets(reach):
        if offset == 0:
            columns.append(jnp.ones(block_ids.shape, dtype=bool))
        else:
            target = (block_ids + offset) % blocks
            columns.append(jnp.any((pair_blocks == target[:, None]) & used, axis=1))
    return jnp.stack(columns, axis=1)


def scores_of(query_rows, passage_rows):
    plain_similarities = lax.dot_general(query_rows, passage_rows, (((1,), (1,)), ((), ())), preferred_element_type=jnp.float32)
    return logit_multiplier * plain_similarities


def partial_stats(scores):
    row_top = jnp.max(scores, axis=1)
    line_exponential_sum = jnp.sum(jnp.exp(scores - row_top[:, None]), axis=1)
    col_top = jnp.max(scores, axis=0)
    col_total = jnp.sum(jnp.exp(scores - col_top[None, :]), axis=0)
    return row_top, line_exponential_sum, col_top, col_total


def merge_lse(tops, totals):
    top = jnp.max(tops, axis=0)
    return top + jnp.log(jnp.sum(totals * jnp.exp(tops - top), axis=0))


def weight_of(scores, row_lse, col_lse, present_markers, diagonal):
    similarity_gap = jnp.exp(scores - row_lse[:, None]) + jnp.exp(scores - col_lse[None, :])
    if diagonal is not None:
        similarity_gap = similarity_gap - 2.0 * diagonal
    return jnp.where(present_markers, logit_multiplier * similarity_gap, 0.0).astype(jnp.bfloat16)


def reference(queries, passages, positives, pair_blocks, negative_pair_count):
    query_blocks = queries.reshape(NB, BLK, D)
    passage_blocks = passages.reshape(NB, BLK, D)
    block_ids = jnp.arange(NB, dtype=jnp.int32)
    mask = slot_mask(pair_blocks, negative_pair_count, block_ids, NB, RANGE)
    offsets = slot_offsets(RANGE)
    columns = jnp.arange(BLK, dtype=jnp.int32)

    def first(block):
        query_rows = query_blocks[block]
        diagonal = (positives[block][:, None] == columns[None, :]).astype(jnp.float32)
        tops, totals, col_tops, col_totals = [], [], [], []
        row_pos = None
        col_pos = None
        for slot, offset in enumerate(offsets):
            target = (block + offset) % NB
            scores = scores_of(query_rows, passage_blocks[target])
            row_top, line_exponential_sum, col_top, col_total = partial_stats(scores)
            present_markers = mask[block, slot]
            tops.append(jnp.where(present_markers, row_top, far_negative))
            totals.append(jnp.where(present_markers, line_exponential_sum, 0.0))
            col_tops.append(jnp.where(present_markers, col_top, far_negative))
            col_totals.append(jnp.where(present_markers, col_total, 0.0))
            if offset == 0:
                row_pos = jnp.sum(scores * diagonal, axis=1)
                col_pos = jnp.sum(scores * diagonal, axis=0)
        row_lse = merge_lse(jnp.stack(tops), jnp.stack(totals))
        return row_lse, row_pos, col_pos, jnp.stack(col_tops), jnp.stack(col_totals)

    row_lse, row_pos, col_pos, col_tops, col_totals = lax.map(first, block_ids)
    shifted_tops = jnp.stack([jnp.roll(col_tops[:, slot], offset, axis=0) for slot, offset in enumerate(offsets)])
    shifted_totals = jnp.stack([jnp.roll(col_totals[:, slot], offset, axis=0) for slot, offset in enumerate(offsets)])
    col_lse = merge_lse(shifted_tops, shifted_totals)
    query_loss = row_lse - row_pos
    passage_loss = col_lse - col_pos

    def latter_operand(passage_grad, block):
        query_rows = query_blocks[block]
        diagonal = (positives[block][:, None] == columns[None, :]).astype(jnp.float32)
        query_grad = jnp.zeros((BLK, D), jnp.float32)
        for slot, offset in enumerate(offsets):
            target = (block + offset) % NB
            passage_rows = passage_blocks[target]
            scores = scores_of(query_rows, passage_rows)
            weight = weight_of(scores, row_lse[block], col_lse[target], mask[block, slot], diagonal if offset == 0 else None)
            query_grad = query_grad + jnp.dot(weight, passage_rows, preferred_element_type=jnp.float32)
            term = lax.dot_general(weight, query_rows, (((0,), (0,)), ((), ())), preferred_element_type=jnp.float32)
            passage_grad = passage_grad.at[target].add(term)
        return passage_grad, query_grad

    passage_grad, query_grad = lax.scan(latter_operand, jnp.zeros((NB, BLK, D), jnp.float32), block_ids)
    return query_loss, passage_loss, query_grad.reshape(ROWS, D), passage_grad.reshape(ROWS, D)
```

```python
import jax
import jax.numpy as jnp
from jax import lax
from jax.sharding import PartitionSpec as P

AXES = ("dp", "cores")
LOGIT = 20.0
FAR = -1e30
SLOTS = dict(own=0, s0=1, a=2, sa=-1, r2=4, s2=-3, b=-2, sb=3, r3=-4)
NAMES = tuple(SLOTS)


def split(value, by_core0, by_core1):
    n = lax.axis_size(AXES)
    pairs = [(i, (i + 2 * (by_core1 if i % 2 else by_core0)) % n) for i in range(n)]
    return lax.ppermute(value, AXES, pairs)


def swap(value):
    n = lax.axis_size(AXES)
    return lax.ppermute(value, AXES, [(i, i ^ 1) for i in range(n)])


def after(value, *others):
    return lax.optimization_barrier((value,) + others)[0]


def halo(own, first):
    got = dict(own=own)
    own = after(own, *first) if first else own
    got["a"] = split(own, -1, 1)
    got["s0"] = swap(own)
    got["r2"] = split(got["a"], -1, 1)
    got["sa"] = swap(got["a"])
    got["b"] = split(after(own, got["r2"]), 1, -1)
    got["r3"] = split(got["r2"], 4, -4)
    got["s2"] = swap(got["r2"])
    got["sb"] = swap(got["b"])
    return got


def scores_of(rows, columns):
    return LOGIT * lax.dot_general(
        rows, columns, (((1,), (1,)), ((), ())), preferred_element_type=jnp.float32
    )


def partial_stats(scores):
    row_top = jnp.max(scores, axis=1)
    row_total = jnp.sum(jnp.exp(scores - row_top[:, None]), axis=1)
    col_top = jnp.max(scores, axis=0)
    col_total = jnp.sum(jnp.exp(scores - col_top[None, :]), axis=0)
    return jnp.stack([row_top, row_total]), jnp.stack([col_top, col_total])


def merge(*stats):
    tops = jnp.stack([s[0] for s in stats])
    totals = jnp.stack([s[1] for s in stats])
    top = jnp.max(tops, axis=0)
    return jnp.stack([top, jnp.sum(totals * jnp.exp(tops - top), axis=0)])


def lse_of(stat):
    return stat[0] + jnp.log(stat[1])


def term(scores, own_lse, other_lse, present, diagonal, others):
    weight = jnp.exp(scores - own_lse[:, None]) + jnp.exp(scores - other_lse[None, :])
    if diagonal is not None:
        weight = weight - 2.0 * diagonal
    weight = jnp.where(present, LOGIT * weight, 0.0).astype(jnp.bfloat16)
    return jnp.dot(weight, others, preferred_element_type=jnp.float32)


def body(queries, passages, positives, pair_blocks, negative_pair_count):
    blocks = lax.axis_size(AXES)
    core = lax.axis_index("cores")
    block = lax.axis_index(AXES)
    rows = queries.shape[0]
    used = jnp.arange(pair_blocks.shape[1], dtype=jnp.int32) < negative_pair_count[0]
    present = {}
    for name, offset in SLOTS.items():
        target = (block + jnp.where(core == 0, offset, -offset)) % blocks
        present[name] = jnp.any((pair_blocks[0] == target) & used) if offset else jnp.array(True)

    ps = halo(passages, ())
    qs = halo(queries, (ps["b"],))

    scores, row_stats, col_stats = {}, {}, {}
    for name in NAMES:
        scores[name] = scores_of(queries, ps[name])
        row, col = partial_stats(scores[name])
        absent = jnp.array([[FAR], [0.0]], jnp.float32)
        row_stats[name] = jnp.where(present[name], row, absent)
        col_stats[name] = jnp.where(present[name], col, absent)
    row_lse = lse_of(merge(*row_stats.values()))

    from_peer = swap(jnp.stack([col_stats[name] for name in ("s0", "sa", "sb", "s2")]))
    own_stat = [col_stats["own"], from_peer[0]]
    own_stat.append(split(merge(col_stats["a"], from_peer[1]), 1, -1))
    own_stat.append(split(merge(col_stats["b"], from_peer[2]), -1, 1))
    own_stat.append(split(merge(col_stats["r2"], from_peer[3]), 2, -2))
    own_stat.append(split(col_stats["r3"], -2, 2))
    col_lse = lse_of(merge(*own_stat))

    offsets = list(range(-4, 5))
    flags = jnp.zeros((rows,), jnp.float32)
    for name, offset in SLOTS.items():
        flag = present[name].astype(jnp.float32)
        flags = flags.at[4 + offset].set(jnp.where(core == 0, flag, flags[4 + offset]))
        flags = flags.at[4 - offset].set(jnp.where(core == 1, flag, flags[4 - offset]))
    pay = jnp.stack([row_lse, col_lse, flags])
    far = dict(
        own=pay, a=split(pay, -1, 1), b=split(pay, 1, -1), r2=split(pay, -2, 2), r3=split(pay, 2, -2)
    )
    peer = swap(jnp.stack([pay, far["a"], far["b"], far["r2"]]))
    for i, name in enumerate(("s0", "sa", "sb", "s2")):
        far[name] = peer[i]

    columns = jnp.arange(rows, dtype=jnp.int32)
    diagonal = (positives[0][:, None] == columns[None, :]).astype(jnp.float32)
    row_pos = jnp.sum(scores["own"] * diagonal, axis=1)
    col_pos = jnp.sum(scores["own"] * diagonal, axis=0)

    query_grad = None
    for name in NAMES:
        part = term(
            scores[name], row_lse, far[name][1], present[name],
            diagonal if name == "own" else None, ps[name],
        )
        query_grad = part if query_grad is None else query_grad + part
    passage_grad = None
    for name in NAMES:
        offset = SLOTS[name]
        flag = jnp.where(core == 0, far[name][2, 4 - offset], far[name][2, 4 + offset]) > 0.5
        part = term(
            scores_of(passages, qs[name]), col_lse, far[name][0], flag,
            diagonal.T if name == "own" else None, qs[name],
        )
        passage_grad = part if passage_grad is None else passage_grad + part
    query_loss = (row_lse - row_pos)[None, :]
    passage_loss = (col_lse - col_pos)[None, :]
    return (query_loss, passage_loss, query_grad, passage_grad)


def solution(mesh):
    spec = P(AXES, None)
    return jax.shard_map(
        body,
        mesh=mesh,
        in_specs=(spec, spec, spec, spec, P(AXES)),
        out_specs=(spec, spec, spec, spec),
        check_vma=False,
    )
```

```python
import functools

import jax
import jax.numpy as jnp
from jax import lax
from jax.experimental import pallas as pl
from jax.experimental.pallas import tpu as pltpu
from jax.sharding import PartitionSpec as P

AXES = ("dp", "cores")
LOGIT = 20.0
FAR = -1e30
BLK = 512
WIDTH = 1024
MIB = 1 << 20
SLOTS = dict(own=0, s0=1, a=2, sa=-1, r2=4, s2=-3, b=-2, sb=3, r3=-4)
NAMES = tuple(SLOTS)
PLACE = {name: i for i, name in enumerate(NAMES)}
BACK = dict(own="own", s0="s0", a="b", b="a", r2="r3", r3="r2", sa="sa", sb="sb", s2="s2")
FREE = pl.CostEstimate(flops=0, bytes_accessed=0, transcendentals=0)
LIMIT = pltpu.CompilerParams(vmem_limit_bytes=16 * MIB)


def split(value, by_core0, by_core1):
    n = lax.axis_size(AXES)
    pairs = [(i, (i + 2 * (by_core1 if i % 2 else by_core0)) % n) for i in range(n)]
    return lax.ppermute(value, AXES, pairs)


def swap(value):
    n = lax.axis_size(AXES)
    return lax.ppermute(value, AXES, [(i, i ^ 1) for i in range(n)])


def after(value, *others):
    return lax.optimization_barrier((value,) + others)[0]


def column_of(row):
    return jnp.transpose(jnp.broadcast_to(row, (128, row.shape[1])))[:, 0:1]


def rows_of(*columns):
    lane = lax.broadcasted_iota(jnp.int32, (columns[0].shape[0], 128), 1)
    packed = jnp.zeros(lane.shape, jnp.float32)
    for i, column in enumerate(columns):
        packed = jnp.where(lane == i, column, packed)
    return jnp.transpose(packed)[0:8]


def scores_of(rows, columns):
    return LOGIT * lax.dot_general(
        rows, columns, (((1,), (1,)), ((), ())), preferred_element_type=jnp.float32
    )


VMEM = pl.BlockSpec(memory_space=pltpu.VMEM)
SMEM = pl.BlockSpec(memory_space=pltpu.SMEM)
HBM = pl.BlockSpec(memory_space=pltpu.HBM)
DMA = pltpu.SemaphoreType.DMA


def small(*lead):
    return jax.ShapeDtypeStruct(lead + (8, BLK), jnp.float32)


def stats_kernel(names, passage_side, *refs):
    n = len(names)
    positives, rows = refs[:2]
    others = refs[2 : 2 + n]
    scores, stats = refs[2 + n :]
    for i, name in enumerate(names):
        s = scores_of(rows[...], others[i][...])
        scores[i] = s
        row_top = jnp.max(s, axis=1, keepdims=True)
        columns = [row_top, jnp.sum(jnp.exp(s - row_top), axis=1, keepdims=True)]
        row = None
        if name == "own" and not passage_side:
            lanes = lax.broadcasted_iota(jnp.int32, s.shape, 1)
            chosen = column_of(positives[...].astype(jnp.float32)).astype(jnp.int32)
            hit = jnp.where(lanes == chosen, s, 0.0)
            columns.append(jnp.sum(hit, axis=1, keepdims=True))
            row = jnp.sum(hit, axis=0, keepdims=True)
        stats[i] = rows_of(*columns)
        if row is not None:
            stats[i, 3:4] = row


def stats_of(names, passage_side, positives, rows, others):
    n = len(names)
    return pl.pallas_call(
        functools.partial(stats_kernel, names, passage_side),
        in_specs=[VMEM] * (2 + n),
        out_specs=[VMEM, VMEM],
        out_shape=[jax.ShapeDtypeStruct((n, BLK, BLK), jnp.float32), small(n)],
        compiler_params=LIMIT,
        cost_estimate=FREE,
        name="stats_" + names[0],
    )(positives, rows, *others)


GROUPS = (("own", "s0"), ("a", "sa"), ("b", "sb"), ("r2", "r3", "s2"))
ORDER = sum(GROUPS, ())
SPOT = {name: (g, i) for g, names in enumerate(GROUPS) for i, name in enumerate(names)}


def message_of(name, messages):
    message, which = MESSAGE[name]
    return messages[MESSAGES.index(message)].at[which]


def present_of(name, messages, lane):
    flags = message_of(name, messages)[1:2]
    lanes = jnp.where(lane == PLACE[BACK[name]], flags, 0.0)
    return jnp.broadcast_to(jnp.sum(lanes, axis=1, keepdims=True), lane.shape) > 0.5


def lse_kernel(passage_side, *refs):
    flags, stats, own_scores, refs = refs[0], refs[1:5], refs[5], refs[6:]
    messages, refs = (refs[:5], refs[5:]) if passage_side else ((), refs)
    pay, loss = refs
    lane = lax.broadcasted_iota(jnp.int32, (1, BLK), 1)
    tops, totals = [], []
    for name in ORDER:
        g, i = SPOT[name]
        top, total = stats[g][i, 0:1], stats[g][i, 1:2]
        if name != "own":
            here = present_of(name, messages, lane) if passage_side else flags[PLACE[name]] > 0
            top, total = jnp.where(here, top, FAR), jnp.where(here, total, 0.0)
        tops.append(top)
        totals.append(total)
    top = functools.reduce(jnp.maximum, tops)
    total = sum(total * jnp.exp(t - top) for t, total in zip(tops, totals))
    lse = top + jnp.log(total)
    loss[...] = lse - (own_scores[0, 3:4] if passage_side else own_scores[0, 2:3])
    here = jnp.zeros((1, BLK), jnp.float32)
    for i in range(9):
        here = jnp.where(lane == i, flags[i].astype(jnp.float32), here)
    pay[...] = jnp.zeros(pay.shape, jnp.float32)
    pay[0:1] = lse
    pay[1:2] = here


def lse_of(passage_side, flags, stats, own_scores, messages=()):
    return pl.pallas_call(
        functools.partial(lse_kernel, passage_side),
        in_specs=[SMEM] + [VMEM] * (5 + len(messages)),
        out_specs=[VMEM, VMEM],
        out_shape=[small(), jax.ShapeDtypeStruct((1, BLK), jnp.float32)],
        compiler_params=LIMIT,
        cost_estimate=FREE,
        name="lse_p" if passage_side else "lse_q",
    )(flags, *stats, own_scores, *messages)


def pair_kernel(mine, peer, out):
    out[0] = mine[...]
    out[1] = peer[...]


def pair(mine, peer):
    return pl.pallas_call(
        pair_kernel,
        in_specs=[VMEM, VMEM],
        out_specs=VMEM,
        out_shape=small(2),
        compiler_params=LIMIT,
        cost_estimate=FREE,
        name="pair",
    )(mine, peer)


def exchanged(pay):
    both = pair(pay, swap(pay))
    return [both, split(both, -1, 1), split(both, 1, -1), split(both, -2, 2), split(both, 2, -2)]


MESSAGE = dict(
    own=("pair", 0), s0=("pair", 1), a=("a", 0), sb=("a", 1), b=("b", 0), sa=("b", 1), r2=("r2", 0),
    r3=("r3", 0), s2=("r3", 1),
)
MESSAGES = ("pair", "a", "b", "r2", "r3")


def grad_kernel(passage_side, *refs):
    n = len(ORDER)
    flags, positives, pay = refs[:3]
    messages = refs[3:8]
    scores = refs[8:12]
    others = refs[12 : 12 + n]
    out, total, out_sem = refs[12 + n :]
    own_lse = column_of(pay[0:1])
    lane = lax.broadcasted_iota(jnp.int32, (1, BLK), 1)
    sent = []
    for i, name in enumerate(ORDER):
        g, k = SPOT[name]
        s = scores[g][k]
        other_lse = message_of(name, messages)[0:1]
        weight = jnp.exp(s - own_lse) + jnp.exp(s - other_lse)
        if name == "own":
            if passage_side:
                hit = lax.broadcasted_iota(jnp.int32, s.shape, 0) == positives[...]
            else:
                chosen = column_of(positives[...].astype(jnp.float32)).astype(jnp.int32)
                hit = lax.broadcasted_iota(jnp.int32, s.shape, 1) == chosen
            weight = LOGIT * jnp.where(hit, weight - 2.0, weight)
        else:
            here = present_of(name, messages, lane) if passage_side else flags[PLACE[name]] > 0
            weight = jnp.where(here, LOGIT * weight, 0.0)
        weight = weight.astype(jnp.bfloat16)
        step = WIDTH // 4 if i == n - 1 else WIDTH
        for start in range(0, WIDTH, step):
            span = slice(start, start + step)
            part = jnp.dot(weight, others[i][:, span], preferred_element_type=jnp.float32)
            if i == 0:
                total[:, span] = part
            else:
                total[:, span] += part
            if i == n - 1:
                copy = pltpu.make_async_copy(total.at[:, span], out.at[:, span], out_sem.at[start // step])
                copy.start()
                sent.append(copy)
    for copy in sent:
        copy.wait()


def grad(passage_side, flags, positives, pay, messages, scores, others):
    n = len(ORDER)
    return pl.pallas_call(
        functools.partial(grad_kernel, passage_side),
        in_specs=[SMEM] + [VMEM] * (11 + n),
        out_specs=HBM,
        out_shape=jax.ShapeDtypeStruct((BLK, WIDTH), jnp.float32),
        scratch_shapes=[pltpu.VMEM((BLK, WIDTH), jnp.float32), DMA((4,))],
        compiler_params=LIMIT,
        cost_estimate=FREE,
        name="grad_p" if passage_side else "grad_q",
    )(flags, positives, pay, *messages, *scores, *[others[name] for name in ORDER])


def body(queries, passages, positives, pair_blocks, negative_pair_count):
    blocks = lax.axis_size(AXES)
    sign = 1 - 2 * lax.axis_index("cores")
    offsets = jnp.array([SLOTS[name] for name in NAMES], jnp.int32)
    targets = (lax.axis_index(AXES) + sign * offsets) % blocks
    used = jnp.arange(pair_blocks.shape[1], dtype=jnp.int32) < negative_pair_count[0]
    listed = jnp.any((pair_blocks == targets[:, None]) & used[None, :], axis=1)
    flags = (listed | (offsets == 0)).astype(jnp.int32)

    v = dict(flags=flags, pos=positives, p_own=passages, q_own=queries)

    def stat(side, g):
        rows = v["q_own" if side == "p" else "p_own"]
        others = [v[side + "_" + name] for name in GROUPS[g]]
        v["%s_scores%d" % (side, g)], v["%s_stats%d" % (side, g)] = stats_of(
            GROUPS[g], side == "q", v["pos"], rows, others
        )

    def fence():
        keys = sorted(v)
        v.update(zip(keys, lax.optimization_barrier(tuple(v[key] for key in keys))))

    def listed_of(what):
        return [v["%s%d" % (what, g)] for g in range(4)]

    v["p_a"], v["p_b"] = split(v["p_own"], -1, 1), split(v["p_own"], 1, -1)
    v["p_s0"], v["q_s0"] = swap(v["p_own"]), swap(v["q_own"])
    fence()
    v["p_r2"], v["p_r3"] = split(v["p_a"], -1, 1), split(v["p_b"], 1, -1)
    v["p_sa"], v["p_sb"] = swap(v["p_a"]), swap(v["p_b"])
    stat("p", 0)
    q_a, q_b = split(v["q_own"], -1, 1), split(v["q_own"], 1, -1)
    stat("q", 0)
    stat("p", 1)
    stat("p", 2)
    fence()
    v["p_s2"] = swap(v["p_r2"])
    stat("p", 3)
    v["q_pay"], query_loss = lse_of(False, v["flags"], listed_of("p_stats"), v["p_stats0"])
    from_queries = exchanged(v["q_pay"])
    for i in range(5):
        v["m%d" % i] = from_queries[i]
    v["q_a"], v["q_b"] = q_a, q_b
    fence()
    v["q_r2"], v["q_r3"] = split(v["q_a"], -1, 1), split(v["q_b"], 1, -1)
    v["q_sa"], v["q_sb"] = swap(v["q_a"]), swap(v["q_b"])
    stat("q", 1)
    stat("q", 2)
    fence()
    from_queries = [v["m%d" % i] for i in range(5)]
    v["q_s2"] = swap(v["q_r2"])
    stat("q", 3)
    v["p_pay"], passage_loss = lse_of(
        True, v["flags"], listed_of("q_stats"), v["p_stats0"], from_queries
    )
    from_passages = exchanged(v["p_pay"])
    p_blocks = {name: v["p_" + name] for name in ORDER}
    q_blocks = {name: v["q_" + name] for name in ORDER}
    passage_grad = grad(
        True, v["flags"], v["pos"], v["p_pay"], from_queries, listed_of("q_scores"), q_blocks
    )
    query_grad = grad(
        False, v["flags"], v["pos"], v["q_pay"], from_passages, listed_of("p_scores"), p_blocks
    )
    return (query_loss, passage_loss, query_grad, passage_grad)


def solution(mesh):
    spec = P(AXES, None)
    return jax.shard_map(
        body,
        mesh=mesh,
        in_specs=(spec, spec, spec, spec, P(AXES)),
        out_specs=(spec, spec, spec, spec),
        check_vma=False,
    )
```

```python
import functools

import jax
import jax.numpy as jnp
from jax import lax
from jax.experimental import pallas as pl
from jax.experimental.pallas import tpu as pltpu
from jax.sharding import PartitionSpec as P

AXES = ("dp", "cores")
LOGIT = 20.0
FAR = -1e30
BLK = 512
WIDTH = 1024
MIB = 1 << 20
SLOTS = dict(own=0, s0=1, a=2, sa=-1, sb=3, b=-2, r2=4, s2=-3, r3=-4)
NAMES = tuple(SLOTS)
GROUPS = (("own", "s0"), ("a", "sa"), ("sb", "b"), ("r2", "s2"), ("r3",))
PLACE = {name: i for i, name in enumerate(NAMES)}
SPOT = {name: (g, i) for g, names in enumerate(GROUPS) for i, name in enumerate(names)}
BACK = dict(own="own", s0="s0", a="b", b="a", r2="r3", r3="r2", sa="sa", sb="sb", s2="s2")
MESSAGE = dict(
    own=(0, 0), s0=(0, 1), b=(1, 0), sa=(1, 1), sb=(2, 0), a=(2, 1), r3=(3, 0), s2=(3, 1), r2=(4, 1)
)

VMEM = pl.BlockSpec(memory_space=pltpu.VMEM)
SMEM = pl.BlockSpec(memory_space=pltpu.SMEM)
HBM = pl.BlockSpec(memory_space=pltpu.HBM)
FREE = pl.CostEstimate(flops=0, bytes_accessed=0, transcendentals=0)
LIMIT = pltpu.CompilerParams(vmem_limit_bytes=16 * MIB)


def split(value, by_core0, by_core1):
    n = lax.axis_size(AXES)
    pairs = [(i, (i + 2 * (by_core1 if i % 2 else by_core0)) % n) for i in range(n)]
    return lax.ppermute(value, AXES, pairs)


def swap(value):
    n = lax.axis_size(AXES)
    return lax.ppermute(value, AXES, [(i, i ^ 1) for i in range(n)])


def after(value, *others):
    return lax.optimization_barrier((value,) + others)[0]


def small(*lead):
    return jax.ShapeDtypeStruct(lead + (8, BLK), jnp.float32)


def call(kernel, name, outs, *operands, first=VMEM):
    return pl.pallas_call(
        kernel,
        in_specs=[first] + [VMEM] * (len(operands) - 1),
        out_specs=jax.tree.map(lambda _: VMEM, outs),
        out_shape=outs,
        compiler_params=LIMIT,
        cost_estimate=FREE,
        name=name,
    )(*operands)


def column_of(row):
    return jnp.transpose(jnp.broadcast_to(row, (128, row.shape[1])))[:, 0:1]


def rows_of(*columns):
    lane = lax.broadcasted_iota(jnp.int32, (columns[0].shape[0], 128), 1)
    packed = jnp.zeros(lane.shape, jnp.float32)
    for i, column in enumerate(columns):
        packed = jnp.where(lane == i, column, packed)
    return jnp.transpose(packed)[0:8]


def scores_of(rows, columns):
    return LOGIT * lax.dot_general(
        rows, columns, (((1,), (1,)), ((), ())), preferred_element_type=jnp.float32
    )


def chosen_of(positives):
    return column_of(positives[...].astype(jnp.float32)).astype(jnp.int32)


def pair_kernel(mine, peer, out):
    out[0] = mine[...]
    out[1] = peer[...]


def pair(mine, peer):
    return call(pair_kernel, "pair", jax.ShapeDtypeStruct((2,) + mine.shape, mine.dtype), mine, peer)


def stats_kernel(names, flags, positives, queries, *refs):
    passages, (scores, stats) = refs[:-2], refs[-2:]
    for i, name in enumerate(names):
        s = scores_of(queries[...], passages[i][...])
        scores[i] = s
        row_top = jnp.max(s, axis=1, keepdims=True)
        row_total = jnp.sum(jnp.exp(s - row_top), axis=1, keepdims=True)
        col_top = jnp.max(s, axis=0, keepdims=True)
        col_total = jnp.sum(jnp.exp(s - col_top), axis=0, keepdims=True)
        if name == "own":
            hit = jnp.where(lax.broadcasted_iota(jnp.int32, s.shape, 1) == chosen_of(positives), s, 0.0)
            packed = rows_of(row_top, row_total, jnp.sum(hit, axis=1, keepdims=True))
            stats[i, 0:2] = packed[0:2]
            stats[i, 2:3] = col_top
            stats[i, 3:4] = col_total
            stats[i, 4:5] = packed[2:3]
            stats[i, 5:6] = jnp.sum(hit, axis=0, keepdims=True)
        else:
            here = flags[PLACE[name]] > 0
            packed = rows_of(row_top, row_total)
            stats[i, 0:1] = jnp.where(here, packed[0:1], FAR)
            stats[i, 1:2] = jnp.where(here, packed[1:2], 0.0)
            stats[i, 2:3] = jnp.where(here, col_top, FAR)
            stats[i, 3:4] = jnp.where(here, col_total, 0.0)


def stats_of(g, flags, positives, queries, passages):
    n = len(GROUPS[g])
    outs = [jax.ShapeDtypeStruct((n, BLK, BLK), jnp.float32), small(n)]
    kernel = functools.partial(stats_kernel, GROUPS[g])
    return call(kernel, "stats%d" % g, outs, flags, positives, queries, *passages, first=SMEM)


def merged(parts, at):
    tops, totals = [p[at : at + 1] for p in parts], [p[at + 1 : at + 2] for p in parts]
    top = functools.reduce(jnp.maximum, tops)
    return top, sum(total * jnp.exp(t - top) for t, total in zip(tops, totals))


def merge_into(out, *parts):
    out[2:3], out[3:4] = merged(parts, 2)


def near_kernel(st1, peer1, st2, peer2, st3, peer3, peer4, out):
    merge_into(out.at[0], st1.at[0], peer1.at[1])
    merge_into(out.at[1], st2.at[0], peer2.at[1])
    merge_into(out.at[2], st3.at[0], peer3.at[1])
    out[3] = peer4[0]


def home_kernel(st0, one, two, mine, theirs):
    merge_into(mine, st0.at[0], one.at[0], two.at[2])
    merge_into(theirs, st0.at[1], one.at[1], two.at[3])


def lse_kernel(flags, *refs):
    stats, mine, peer, pay, query_loss, passage_loss = refs[:5], *refs[5:]
    top, total = merged([stats[SPOT[name][0]].at[SPOT[name][1]] for name in NAMES], 0)
    row_lse = top + jnp.log(total)
    top, total = merged([mine, peer], 2)
    col_lse = top + jnp.log(total)
    query_loss[...] = row_lse - stats[0][0, 4:5]
    passage_loss[...] = col_lse - stats[0][0, 5:6]
    lane = lax.broadcasted_iota(jnp.int32, (1, BLK), 1)
    here = jnp.zeros((1, BLK), jnp.float32)
    for i in range(9):
        here = jnp.where(lane == i, flags[i].astype(jnp.float32), here)
    pay[0:1] = row_lse
    pay[1:2] = col_lse
    pay[2:3] = here


def block_of(arrays, spot):
    return arrays[spot[0]] if spot[1] is None else arrays[spot[0]].at[spot[1]]


def tscores_kernel(passages, queries, out):
    for i in range(out.shape[0]):
        out[i] = scores_of(passages[...], queries[i])


def tscores_of(passages, queries):
    out = jax.ShapeDtypeStruct((queries.shape[0], BLK, BLK), jnp.float32)
    return call(tscores_kernel, "tscores", out, passages, queries)


def grad_kernel(names, passage_side, at, scores_at, has_total, sizes, *refs):
    n = len(names)
    flags, positives = refs[:2]
    messages, refs = refs[2:7], refs[7:]
    others, refs = refs[: sizes[0]], refs[sizes[0] :]
    scores, refs = refs[: sizes[1]], refs[sizes[1] :]
    if not scores:
        own, refs = refs[0], refs[1:]
    if has_total:
        earlier, refs = refs[0], refs[1:]
    out, total, out_sem = refs
    own_lse = column_of(messages[0][0, 1:2] if passage_side else messages[0][0, 0:1])
    lane = lax.broadcasted_iota(jnp.int32, (1, BLK), 1)
    sent = []
    for i, name in enumerate(names):
        message, which = MESSAGE[name]
        pay = messages[message].at[which]
        other = block_of(others, at[i])
        s = block_of(scores, scores_at[i])[...] if scores else scores_of(own[...], other[...])
        weight = jnp.exp(s - own_lse) + jnp.exp(s - (pay[0:1] if passage_side else pay[1:2]))
        if name == "own":
            if passage_side:
                hit = lax.broadcasted_iota(jnp.int32, s.shape, 0) == positives[...]
            else:
                hit = lax.broadcasted_iota(jnp.int32, s.shape, 1) == chosen_of(positives)
            weight = LOGIT * jnp.where(hit, weight - 2.0, weight)
        else:
            if passage_side:
                lanes = jnp.where(lane == PLACE[BACK[name]], pay[2:3], 0.0)
                here = jnp.broadcast_to(jnp.sum(lanes, axis=1, keepdims=True), lane.shape) > 0.5
            else:
                here = flags[PLACE[name]] > 0
            weight = jnp.where(here, LOGIT * weight, 0.0)
        weight = weight.astype(jnp.bfloat16)
        last = i == n - 1
        step = WIDTH // 4 if last else WIDTH
        for start in range(0, WIDTH, step):
            span = slice(start, start + step)
            part = jnp.dot(weight, other[:, span], preferred_element_type=jnp.float32)
            if i > 0:
                total[:, span] += part
            else:
                total[:, span] = earlier[:, span] + part if has_total else part
            if last:
                copy = pltpu.make_async_copy(total.at[:, span], out.at[:, span], out_sem.at[start // step])
                copy.start()
                sent.append(copy)
    for copy in sent:
        copy.wait()


def grad(names, passage_side, flags, positives, messages, others, at, scores=(), scores_at=(), own=None, earlier=None):
    operands = [flags, positives, *messages, *others, *scores]
    operands += [] if scores else [own]
    operands += [] if earlier is None else [earlier]
    sizes = (len(others), len(scores))
    return pl.pallas_call(
        functools.partial(grad_kernel, names, passage_side, at, scores_at, earlier is not None, sizes),
        in_specs=[SMEM] + [VMEM] * (len(operands) - 1),
        out_specs=HBM,
        out_shape=jax.ShapeDtypeStruct((BLK, WIDTH), jnp.float32),
        scratch_shapes=[pltpu.VMEM((BLK, WIDTH), jnp.float32), pltpu.SemaphoreType.DMA((4,))],
        compiler_params=LIMIT,
        cost_estimate=FREE,
        name="grad_" + ("p_" if passage_side else "q_") + names[0],
    )(*operands)


def body(queries, passages, positives, pair_blocks, negative_pair_count):
    blocks = lax.axis_size(AXES)
    sign = 1 - 2 * lax.axis_index("cores")
    offsets = jnp.array([SLOTS[name] for name in NAMES], jnp.int32)
    targets = (lax.axis_index(AXES) + sign * offsets) % blocks
    used = jnp.arange(pair_blocks.shape[1], dtype=jnp.int32) < negative_pair_count[0]
    listed = jnp.any((pair_blocks == targets[:, None]) & used[None, :], axis=1)
    flags = (listed | (offsets == 0)).astype(jnp.int32)

    v = dict(flags=flags, pos=positives, q=queries, p=passages)

    def fence():
        keys = sorted(v)
        v.update(zip(keys, lax.optimization_barrier(tuple(v[key] for key in keys))))

    def stat(g):
        v["s%d" % g], v["st%d" % g] = stats_of(
            g, v["flags"], v["pos"], v["q"], [v["p_" + name] for name in GROUPS[g]]
        )

    def group_of(what):
        return [v["%s%d" % (what, g)] for g in range(5)]

    v["p_own"] = v.pop("p")
    v["p_s0"], v["q_s0"] = swap(v["p_own"]), swap(v["q"])
    v["p_a"], v["p_sb"] = split(v["p_own"], -1, 1), split(v["p_s0"], -1, 1)
    stat(0)
    fence()
    p_r2, p_r4 = split(v["p_a"], -1, 1), split(v["p_sb"], -1, 1)
    v["p_sa"], v["p_b"] = swap(v["p_a"]), swap(v["p_sb"])
    stat(1)
    stat(2)
    v["x1"], v["x2"] = swap(v["st1"]), swap(v["st2"])
    v["q0"] = pair(v["q"], v["q_s0"])
    q1 = split(after(v["q0"], v["st1"]), -1, 1)
    v["p_r2"], v["p_r4"] = p_r2, p_r4
    fence()
    v["p_s2"], v["p_r3"] = swap(v["p_r2"]), swap(v["p_r4"])
    stat(3)
    stat(4)
    x3, x4 = swap(v["st3"]), swap(v["st4"])
    near = call(near_kernel, "near", small(4), v["st1"], v["x1"], v["st2"], v["x2"], v["st3"], x3, x4)
    v["one"] = split(near, 1, -1)
    v["two"] = split(v["one"], 1, -1)
    v["t0"] = tscores_of(v["p_own"], v["q0"])
    v["q1"] = q1
    fence()
    v["q3"] = split(v["q1"], -1, 1)
    v["q2"] = swap(v["q1"])
    mine, theirs = call(home_kernel, "home", [small()] * 2, v["st0"], v["one"], v["two"])
    line = jax.ShapeDtypeStruct((1, BLK), jnp.float32)
    pay, query_loss, passage_loss = call(
        lse_kernel, "lse", [small(), line, line], v["flags"], *group_of("st"), mine, swap(theirs), first=SMEM
    )
    m0 = pair(pay, swap(pay))
    m1 = split(m0, 1, -1)
    m3 = split(m1, 1, -1)
    messages = [m0, m1, swap(m1), m3, swap(m3)]
    query_grad = grad(
        NAMES, False, v["flags"], v["pos"], messages, [v["p_" + name] for name in NAMES],
        [(i, None) for i in range(9)], group_of("s"), [SPOT[name] for name in NAMES],
    )
    early, late = ("own", "s0", "a", "sb", "sa", "b"), ("r2", "s2", "r3")
    spots = [(i // 2, i % 2) for i in range(6)]
    scores = [v["t0"], tscores_of(v["p_own"], v["q1"]), tscores_of(v["p_own"], v["q2"])]
    total = grad(
        early, True, v["flags"], v["pos"], messages, [v["q0"], v["q1"], v["q2"]], spots, scores, spots
    )
    q4 = swap(after(v["q3"], query_grad))
    passage_grad = grad(
        late, True, v["flags"], v["pos"], messages, [v["q3"], q4], [(0, 0), (1, 0), (1, 1)],
        own=v["p_own"], earlier=total,
    )
    return (query_loss, passage_loss, query_grad, passage_grad)


def solution(mesh):
    spec = P(AXES, None)
    return jax.shard_map(
        body,
        mesh=mesh,
        in_specs=(spec, spec, spec, spec, P(AXES)),
        out_specs=(spec, spec, spec, spec),
        check_vma=False,
    )
```

```python
import functools

import jax
import jax.numpy as jnp
from jax import lax
from jax.experimental import pallas as pl
from jax.experimental.pallas import tpu as pltpu
from jax.sharding import PartitionSpec as P

AXES = ("dp", "cores")
LOGIT = 20.0
FAR = -1e30
BLK = 512
WIDTH = 1024
MIB = 1 << 20
SLOTS = dict(own=0, s0=1, a=2, sa=-1, sb=3, b=-2, r2=4, s2=-3, r3=-4)
NAMES = tuple(SLOTS)
GROUPS = (("own", "s0"), ("a", "sa"), ("sb", "b"), ("r2", "s2"), ("r3",))
PLACE = {name: i for i, name in enumerate(NAMES)}
SPOT = {name: (g, i) for g, names in enumerate(GROUPS) for i, name in enumerate(names)}
BACK = dict(own="own", s0="s0", a="b", b="a", r2="r3", r3="r2", sa="sa", sb="sb", s2="s2")
MESSAGE = dict(
    own=(0, 0), s0=(0, 1), b=(1, 0), sa=(1, 1), sb=(2, 0), a=(2, 1), r3=(3, 0), s2=(3, 1), r2=(4, 1)
)

VMEM = pl.BlockSpec(memory_space=pltpu.VMEM)
SMEM = pl.BlockSpec(memory_space=pltpu.SMEM)
HBM = pl.BlockSpec(memory_space=pltpu.HBM)
FREE = pl.CostEstimate(flops=0, bytes_accessed=0, transcendentals=0)
LIMIT = pltpu.CompilerParams(vmem_limit_bytes=16 * MIB)


def split(value, by_core0, by_core1):
    n = lax.axis_size(AXES)
    pairs = [(i, (i + 2 * (by_core1 if i % 2 else by_core0)) % n) for i in range(n)]
    return lax.ppermute(value, AXES, pairs)


def swap(value):
    n = lax.axis_size(AXES)
    return lax.ppermute(value, AXES, [(i, i ^ 1) for i in range(n)])


def after(value, *others):
    return lax.optimization_barrier((value,) + others)[0]


def small(*lead):
    return jax.ShapeDtypeStruct(lead + (8, BLK), jnp.float32)


def call(kernel, name, outs, *operands, first=VMEM):
    return pl.pallas_call(
        kernel,
        in_specs=[first] + [VMEM] * (len(operands) - 1),
        out_specs=jax.tree.map(lambda _: VMEM, outs),
        out_shape=outs,
        compiler_params=LIMIT,
        cost_estimate=FREE,
        name=name,
    )(*operands)


def column_of(row):
    return jnp.transpose(jnp.broadcast_to(row, (128, row.shape[1])))[:, 0:1]


def rows_of(*columns):
    lane = lax.broadcasted_iota(jnp.int32, (columns[0].shape[0], 128), 1)
    packed = jnp.zeros(lane.shape, jnp.float32)
    for i, column in enumerate(columns):
        packed = jnp.where(lane == i, column, packed)
    return jnp.transpose(packed)[0:8]


def scores_of(rows, columns):
    return LOGIT * lax.dot_general(
        rows, columns, (((1,), (1,)), ((), ())), preferred_element_type=jnp.float32
    )


def chosen_of(positives):
    return column_of(positives[...].astype(jnp.float32)).astype(jnp.int32)


def pair_kernel(mine, peer, out):
    out[0] = mine[...]
    out[1] = peer[...]


def pair(mine, peer):
    return call(pair_kernel, "pair", jax.ShapeDtypeStruct((2,) + mine.shape, mine.dtype), mine, peer)


def stats_kernel(names, flags, positives, queries, *refs):
    passages, (scores, stats) = refs[:-2], refs[-2:]
    for i, name in enumerate(names):
        s = scores_of(queries[...], passages[i][...])
        scores[i] = s
        row_top = jnp.max(s, axis=1, keepdims=True)
        row_total = jnp.sum(jnp.exp(s - row_top), axis=1, keepdims=True)
        col_top = jnp.max(s, axis=0, keepdims=True)
        col_total = jnp.sum(jnp.exp(s - col_top), axis=0, keepdims=True)
        if name == "own":
            hit = jnp.where(lax.broadcasted_iota(jnp.int32, s.shape, 1) == chosen_of(positives), s, 0.0)
            packed = rows_of(row_top, row_total, jnp.sum(hit, axis=1, keepdims=True))
            stats[i, 0:2] = packed[0:2]
            stats[i, 2:3] = col_top
            stats[i, 3:4] = col_total
            stats[i, 4:5] = packed[2:3]
            stats[i, 5:6] = jnp.sum(hit, axis=0, keepdims=True)
        else:
            here = flags[PLACE[name]] > 0
            packed = rows_of(row_top, row_total)
            stats[i, 0:1] = jnp.where(here, packed[0:1], FAR)
            stats[i, 1:2] = jnp.where(here, packed[1:2], 0.0)
            stats[i, 2:3] = jnp.where(here, col_top, FAR)
            stats[i, 3:4] = jnp.where(here, col_total, 0.0)


def stats_of(g, flags, positives, queries, passages):
    n = len(GROUPS[g])
    outs = [jax.ShapeDtypeStruct((n, BLK, BLK), jnp.float32), small(n)]
    kernel = functools.partial(stats_kernel, GROUPS[g])
    return call(kernel, "stats%d" % g, outs, flags, positives, queries, *passages, first=SMEM)


def merged(parts, at):
    tops, totals = [p[at : at + 1] for p in parts], [p[at + 1 : at + 2] for p in parts]
    top = functools.reduce(jnp.maximum, tops)
    return top, sum(total * jnp.exp(t - top) for t, total in zip(tops, totals))


def merge_into(out, *parts):
    out[2:3], out[3:4] = merged(parts, 2)


def lse_q_kernel(flags, *refs):
    stats, (pay, loss) = refs[:5], refs[5:]
    top, total = merged([stats[SPOT[name][0]].at[SPOT[name][1]] for name in NAMES], 0)
    lse = top + jnp.log(total)
    lane = lax.broadcasted_iota(jnp.int32, (1, BLK), 1)
    here = jnp.zeros((1, BLK), jnp.float32)
    for i in range(9):
        here = jnp.where(lane == i, flags[i].astype(jnp.float32), here)
    pay[0:1] = lse
    pay[1:2] = here
    loss[...] = lse - stats[0][0, 4:5]


def near_kernel(st1, peer1, st2, peer2, st3, peer3, peer4, pay, peer_pay, out):
    merge_into(out.at[0], st1.at[0], peer1.at[1])
    merge_into(out.at[1], st2.at[0], peer2.at[1])
    merge_into(out.at[2], st3.at[0], peer3.at[1])
    out[3] = peer4[0]
    out[4] = pay[...]
    out[5] = peer_pay[...]


def lse_p_kernel(st0, peer0, one, one_peer, two, two_peer, pay, loss):
    parts = [st0.at[0], peer0.at[1], one.at[0], one_peer.at[1], two.at[2], two_peer.at[3]]
    top, total = merged(parts, 2)
    lse = top + jnp.log(total)
    pay[0:1] = lse
    loss[...] = lse - st0[0, 5:6]


def tscores_kernel(passages, queries, out):
    for i in range(out.shape[0]):
        out[i] = scores_of(passages[...], queries[i])


def tscores_of(passages, queries):
    out = jax.ShapeDtypeStruct((queries.shape[0], BLK, BLK), jnp.float32)
    return call(tscores_kernel, "tscores", out, passages, queries)


def parts_kernel(steps, earlier, final, n_arrays, *refs):
    flags, positives, own_rows, own_columns, refs = *refs[:4], refs[4:]
    from_q, from_p, refs = refs[:5], refs[5:10], refs[10:]
    arrays, refs = refs[:n_arrays], refs[n_arrays:]
    sides = sorted(earlier)
    outs, scratch = refs[: len(sides)], refs[len(sides) :]
    totals, sems = {}, {}
    for side, out in zip(sides, outs):
        if final[side]:
            totals[side], sems[side], *scratch = scratch
        else:
            totals[side] = out
    lane = lax.broadcasted_iota(jnp.int32, (1, BLK), 1)
    own_lse = {side: column_of((own_rows if side == "q" else own_columns)[0:1]) for side in sides}
    left = {side: sum(step[0] == side for step in steps) for side in sides}
    begun = set()
    sent = []
    for side, name, block, score in steps:
        message, which = MESSAGE[name]
        pay = from_q[message].at[4 + which] if side == "p" else from_p[message].at[which]
        other = arrays[block[0]] if block[1] is None else arrays[block[0]].at[block[1]]
        if score[1] is None:
            s = scores_of(arrays[score[0]][...], other[...])
        else:
            s = arrays[score[0]][score[1]]
        weight = jnp.exp(s - own_lse[side]) + jnp.exp(s - pay[0:1])
        if name == "own":
            if side == "p":
                hit = lax.broadcasted_iota(jnp.int32, s.shape, 0) == positives[...]
            else:
                hit = lax.broadcasted_iota(jnp.int32, s.shape, 1) == chosen_of(positives)
            weight = LOGIT * jnp.where(hit, weight - 2.0, weight)
        else:
            if side == "p":
                lanes = jnp.where(lane == PLACE[BACK[name]], pay[1:2], 0.0)
                here = jnp.broadcast_to(jnp.sum(lanes, axis=1, keepdims=True), lane.shape) > 0.5
            else:
                here = flags[PLACE[name]] > 0
            weight = jnp.where(here, LOGIT * weight, 0.0)
        weight = weight.astype(jnp.bfloat16)
        left[side] -= 1
        total = totals[side]
        out = left[side] == 0 and final[side]
        step = WIDTH // 4 if out else WIDTH
        for start in range(0, WIDTH, step):
            span = slice(start, start + step)
            part = jnp.dot(weight, other[:, span], preferred_element_type=jnp.float32)
            if side in begun:
                total[:, span] += part
            elif earlier[side] is None:
                total[:, span] = part
            else:
                total[:, span] = arrays[earlier[side]][:, span] + part
            if out:
                sem = sems[side].at[start // step]
                copy = pltpu.make_async_copy(total.at[:, span], outs[sides.index(side)].at[:, span], sem)
                copy.start()
                sent.append(copy)
        begun.add(side)
    for copy in sent:
        copy.wait()


def parts(name, common, from_p, steps, earlier, final=()):
    arrays = []

    def at(spot):
        for i, array in enumerate(arrays):
            if array is spot[0]:
                return i, spot[1]
        arrays.append(spot[0])
        return len(arrays) - 1, spot[1]

    plan = [(side, slot, at(block), at(scores)) for side, slot, block, scores in steps]
    sides = sorted(earlier)
    begin = {side: None if earlier[side] is None else at((earlier[side], None))[0] for side in sides}
    scratch = []
    for side in sides:
        scratch += [pltpu.VMEM((BLK, WIDTH), jnp.float32), pltpu.SemaphoreType.DMA((4,))] * (side in final)
    last = {side: side in final for side in sides}
    return pl.pallas_call(
        functools.partial(parts_kernel, plan, begin, last, len(arrays)),
        in_specs=[SMEM] + [VMEM] * (13 + len(arrays)),
        out_specs=[HBM if last[side] else VMEM for side in sides],
        out_shape=[jax.ShapeDtypeStruct((BLK, WIDTH), jnp.float32)] * len(sides),
        scratch_shapes=scratch,
        compiler_params=LIMIT,
        cost_estimate=FREE,
        name=name,
    )(*common, *from_p, *arrays)


def body(queries, passages, positives, pair_blocks, negative_pair_count):
    blocks = lax.axis_size(AXES)
    sign = 1 - 2 * lax.axis_index("cores")
    offsets = jnp.array([SLOTS[name] for name in NAMES], jnp.int32)
    targets = (lax.axis_index(AXES) + sign * offsets) % blocks
    used = jnp.arange(pair_blocks.shape[1], dtype=jnp.int32) < negative_pair_count[0]
    listed = jnp.any((pair_blocks == targets[:, None]) & used[None, :], axis=1)
    flags = (listed | (offsets == 0)).astype(jnp.int32)

    v = dict(flags=flags, pos=positives, q=queries, p=passages)

    def fence():
        keys = sorted(v)
        v.update(zip(keys, lax.optimization_barrier(tuple(v[key] for key in keys))))

    def stat(g):
        v["s%d" % g], v["st%d" % g] = stats_of(
            g, v["flags"], v["pos"], v["q"], [v["p_" + name] for name in GROUPS[g]]
        )

    def group_of(what):
        return [v["%s%d" % (what, g)] for g in range(5)]

    v["p_own"] = v.pop("p")
    v["p_s0"], v["q_s0"] = swap(v["p_own"]), swap(v["q"])
    p_sb = split(v["p_s0"], -1, 1)
    v["p_a"] = split(v["p_own"], -1, 1)
    stat(0)
    fence()
    p_r2, p_sa = split(v["p_a"], -1, 1), swap(v["p_a"])
    v["p_sb"] = p_sb
    fence()
    p_r4, p_b = split(v["p_sb"], -1, 1), swap(v["p_sb"])
    v["q0"] = pair(v["q"], v["q_s0"])
    v["p_r2"], v["p_sa"] = p_r2, p_sa
    fence()
    stat(1)
    q1 = split(after(v["q0"], v["st1"]), -1, 1)
    v["p_r4"], v["p_b"] = p_r4, p_b
    fence()
    v["p_s2"], v["p_r3"] = swap(v["p_r2"]), swap(v["p_r4"])
    stat(2)
    stat(3)
    stat(4)
    line = jax.ShapeDtypeStruct((1, BLK), jnp.float32)
    q_pay, query_loss = call(lse_q_kernel, "lse_q", [small(), line], v["flags"], *group_of("st"), first=SMEM)
    x0, x1, x2, x3, x4 = (swap(stats) for stats in group_of("st"))
    near = call(
        near_kernel, "near", small(6), v["st1"], x1, v["st2"], x2, v["st3"], x3, x4, q_pay, swap(q_pay)
    )
    v["one"] = split(near, 1, -1)
    v["two"] = split(v["one"], 1, -1)
    v["one_peer"] = swap(v["one"])
    v["x0"], v["near"], v["q_pay"] = x0, near, q_pay
    v["t0"] = tscores_of(v["p_own"], v["q0"])
    v["q1"] = q1
    fence()
    v["q3"] = split(v["q1"], -1, 1)
    v["q2"] = swap(v["q1"])
    two_peer = swap(v["two"])
    p_pay, passage_loss = call(
        lse_p_kernel, "lse_p", [small(), line], v["st0"], v["x0"], v["one"], v["one_peer"], v["two"], two_peer
    )
    m0 = pair(p_pay, swap(p_pay))

    common = (v["flags"], v["pos"], v["q_pay"], p_pay, v["near"], v["one"], v["one_peer"], v["two"], two_peer)
    places = dict(
        own=("q0", 0), s0=("q0", 1), a=("q1", 0), sb=("q1", 1), sa=("q2", 0), b=("q2", 1), r2=("q3", 0),
        s2=("q4", 0), r3=("q4", 1),
    )

    def steps_of(side, *names):
        steps = []
        for name in names:
            if side == "q":
                g, k = SPOT[name]
                steps.append(("q", name, (v["p_" + name], None), (v["s%d" % g], k)))
            else:
                array, k = places[name]
                scores = (v["t0"], k) if array == "q0" else (v["p_own"], None)
                steps.append(("p", name, (v[array], k), scores))
        return steps

    hold = lax.optimization_barrier
    m1 = split(m0, 1, -1)
    steps = steps_of("q", "own", "s0") + steps_of("p", "own", "s0", "sa", "b")
    p_total, q_total = parts("part0", common, [m0] * 5, steps, dict(p=None, q=None))
    m1, q_total, p_total = hold((m1, q_total, p_total))
    m3 = split(m1, 1, -1)
    m2 = swap(m1)
    steps = steps_of("q", "sa", "b") + steps_of("p", "a", "sb")
    p_total, q_total = parts("part1", common, [m0, m1, m0, m0, m0], steps, dict(p=p_total, q=q_total))
    m2, m3, q_total, p_total = hold((m2, m3, q_total, p_total))
    m4 = swap(m3)
    m4, v["q3"] = hold((m4, v["q3"]))
    v["q4"] = swap(v["q3"])
    messages = [m0, m1, m2, m3, m4]
    (query_grad,) = parts(
        "part2", common, messages, steps_of("q", "a", "sb", "s2", "r3", "r2"), dict(q=q_total), "q"
    )
    v["q4"], p_total, _ = hold((v["q4"], p_total, query_grad))
    (passage_grad,) = parts("part3", common, messages, steps_of("p", "r2", "s2", "r3"), dict(p=p_total), "p")
    return (query_loss, passage_loss, query_grad, passage_grad)


def solution(mesh):
    spec = P(AXES, None)
    return jax.shard_map(
        body,
        mesh=mesh,
        in_specs=(spec, spec, spec, spec, P(AXES)),
        out_specs=(spec, spec, spec, spec),
        check_vma=False,
    )
```

```python
import functools

import jax
import jax.numpy as jnp
from jax import lax
from jax.experimental import pallas as pl
from jax.experimental.pallas import tpu as pltpu
from jax.sharding import PartitionSpec as P

AXES = ("dp", "cores")
LOGIT = 20.0
FAR = -1e30
BLK = 512
WIDTH = 1024
MIB = 1 << 20
SLOTS = dict(own=0, s0=1, a=-2, sa=3, sb=-1, b=2, r2=-4, r4=-3, s4=4)
NAMES = tuple(SLOTS)
GROUPS = (("own", "s0"), ("a", "sa"), ("sb", "b"), ("r2", "r4"), ("s4",))
PLACE = {name: i for i, name in enumerate(NAMES)}
SPOT = {name: (g, i) for g, names in enumerate(GROUPS) for i, name in enumerate(names)}
BACK = dict(own="own", s0="s0", a="b", b="a", r2="s4", s4="r2", sa="sa", sb="sb", r4="r4")
MESSAGE = dict(
    own=(0, 0), s0=(0, 1), b=(1, 0), sa=(1, 1), sb=(2, 0), a=(2, 1), s4=(3, 0), r4=(4, 0), r2=(4, 1)
)

VMEM = pl.BlockSpec(memory_space=pltpu.VMEM)
SMEM = pl.BlockSpec(memory_space=pltpu.SMEM)
HBM = pl.BlockSpec(memory_space=pltpu.HBM)
FREE = pl.CostEstimate(flops=0, bytes_accessed=0, transcendentals=0)
LIMIT = pltpu.CompilerParams(vmem_limit_bytes=16 * MIB)


def split(value, by_core0, by_core1):
    n = lax.axis_size(AXES)
    pairs = [(i, (i + 2 * (by_core1 if i % 2 else by_core0)) % n) for i in range(n)]
    return lax.ppermute(value, AXES, pairs)


def swap(value):
    n = lax.axis_size(AXES)
    return lax.ppermute(value, AXES, [(i, i ^ 1) for i in range(n)])


def after(value, *others):
    return lax.optimization_barrier((value,) + others)[0]


def small(*lead):
    return jax.ShapeDtypeStruct(lead + (8, BLK), jnp.float32)


def call(kernel, name, outs, *operands, first=VMEM):
    return pl.pallas_call(
        kernel,
        in_specs=[first] + [VMEM] * (len(operands) - 1),
        out_specs=jax.tree.map(lambda _: VMEM, outs),
        out_shape=outs,
        compiler_params=LIMIT,
        cost_estimate=FREE,
        name=name,
    )(*operands)


def column_of(row):
    return jnp.transpose(jnp.broadcast_to(row, (128, row.shape[1])))[:, 0:1]


def rows_of(*columns):
    lane = lax.broadcasted_iota(jnp.int32, (columns[0].shape[0], 128), 1)
    packed = jnp.zeros(lane.shape, jnp.float32)
    for i, column in enumerate(columns):
        packed = jnp.where(lane == i, column, packed)
    return jnp.transpose(packed)[0:8]


def scores_of(rows, columns):
    return LOGIT * lax.dot_general(
        rows, columns, (((1,), (1,)), ((), ())), preferred_element_type=jnp.float32
    )


def chosen_of(positives):
    return column_of(positives[...].astype(jnp.float32)).astype(jnp.int32)


def pair_kernel(mine, peer, out):
    out[0] = mine[...]
    out[1] = peer[...]


def pair(mine, peer):
    return call(pair_kernel, "pair", jax.ShapeDtypeStruct((2,) + mine.shape, mine.dtype), mine, peer)


def stats_kernel(names, flags, positives, queries, *refs):
    passages, (scores, stats) = refs[:-2], refs[-2:]
    for i, name in enumerate(names):
        s = scores_of(queries[...], passages[i][...])
        scores[i] = s
        row_top = jnp.max(s, axis=1, keepdims=True)
        row_total = jnp.sum(jnp.exp(s - row_top), axis=1, keepdims=True)
        col_top = jnp.max(s, axis=0, keepdims=True)
        col_total = jnp.sum(jnp.exp(s - col_top), axis=0, keepdims=True)
        if name == "own":
            hit = jnp.where(lax.broadcasted_iota(jnp.int32, s.shape, 1) == chosen_of(positives), s, 0.0)
            packed = rows_of(row_top, row_total, jnp.sum(hit, axis=1, keepdims=True))
            stats[i, 0:2] = packed[0:2]
            stats[i, 2:3] = col_top
            stats[i, 3:4] = col_total
            stats[i, 4:5] = packed[2:3]
            stats[i, 5:6] = jnp.sum(hit, axis=0, keepdims=True)
        else:
            here = flags[PLACE[name]] > 0
            packed = rows_of(row_top, row_total)
            stats[i, 0:1] = jnp.where(here, packed[0:1], FAR)
            stats[i, 1:2] = jnp.where(here, packed[1:2], 0.0)
            stats[i, 2:3] = jnp.where(here, col_top, FAR)
            stats[i, 3:4] = jnp.where(here, col_total, 0.0)


def stats_of(g, flags, positives, queries, passages):
    n = len(GROUPS[g])
    outs = [jax.ShapeDtypeStruct((n, BLK, BLK), jnp.float32), small(n)]
    kernel = functools.partial(stats_kernel, GROUPS[g])
    return call(kernel, "stats%d" % g, outs, flags, positives, queries, *passages, first=SMEM)


def merged(parts, at):
    tops, totals = [p[at : at + 1] for p in parts], [p[at + 1 : at + 2] for p in parts]
    top = functools.reduce(jnp.maximum, tops)
    return top, sum(total * jnp.exp(t - top) for t, total in zip(tops, totals))


def merge_into(out, *parts):
    out[2:3], out[3:4] = merged(parts, 2)


def lse_q_kernel(flags, *refs):
    stats, (pay, loss) = refs[:5], refs[5:]
    top, total = merged([stats[SPOT[name][0]].at[SPOT[name][1]] for name in NAMES], 0)
    lse = top + jnp.log(total)
    lane = lax.broadcasted_iota(jnp.int32, (1, BLK), 1)
    here = jnp.zeros((1, BLK), jnp.float32)
    for i in range(9):
        here = jnp.where(lane == i, flags[i].astype(jnp.float32), here)
    pay[0:1] = lse
    pay[1:2] = here
    loss[...] = lse - stats[0][0, 4:5]


def near_kernel(st1, peer1, st2, peer2, st3, peer4, pay, peer_pay, out):
    merge_into(out.at[0], st1.at[0], peer1.at[1])
    merge_into(out.at[1], st2.at[0], peer2.at[1])
    out[2] = st3[0]
    merge_into(out.at[3], st3.at[1], peer4.at[0])
    out[4] = pay[...]
    out[5] = peer_pay[...]


def lse_p_kernel(st0, peer0, one, one_peer, two, two_peer, pay, loss):
    parts = [st0.at[0], peer0.at[1], one.at[0], one_peer.at[1], two.at[2], two_peer.at[3]]
    top, total = merged(parts, 2)
    lse = top + jnp.log(total)
    pay[0:1] = lse
    loss[...] = lse - st0[0, 5:6]


def tscores_kernel(passages, queries, out):
    for i in range(out.shape[0]):
        out[i] = scores_of(passages[...], queries[i])


def tscores_of(passages, queries):
    out = jax.ShapeDtypeStruct((queries.shape[0], BLK, BLK), jnp.float32)
    return call(tscores_kernel, "tscores", out, passages, queries)


def parts_kernel(steps, earlier, final, n_arrays, *refs):
    flags, positives, own_rows, own_columns, refs = *refs[:4], refs[4:]
    from_q, from_p, refs = refs[:5], refs[5:10], refs[10:]
    arrays, refs = refs[:n_arrays], refs[n_arrays:]
    sides = sorted(earlier)
    outs, scratch = refs[: len(sides)], refs[len(sides) :]
    totals, sems = {}, {}
    for side, out in zip(sides, outs):
        if final[side]:
            totals[side], sems[side], *scratch = scratch
        else:
            totals[side] = out
    lane = lax.broadcasted_iota(jnp.int32, (1, BLK), 1)
    own_lse = {side: column_of((own_rows if side == "q" else own_columns)[0:1]) for side in sides}
    left = {side: sum(step[0] == side for step in steps) for side in sides}
    begun = set()
    sent = []
    for side, name, block, score in steps:
        message, which = MESSAGE[name]
        pay = from_q[message].at[4 + which] if side == "p" else from_p[message].at[which]
        other = arrays[block[0]] if block[1] is None else arrays[block[0]].at[block[1]]
        if score[1] is None:
            s = scores_of(arrays[score[0]][...], other[...])
        else:
            s = arrays[score[0]][score[1]]
        weight = jnp.exp(s - own_lse[side]) + jnp.exp(s - pay[0:1])
        if name == "own":
            if side == "p":
                hit = lax.broadcasted_iota(jnp.int32, s.shape, 0) == positives[...]
            else:
                hit = lax.broadcasted_iota(jnp.int32, s.shape, 1) == chosen_of(positives)
            weight = LOGIT * jnp.where(hit, weight - 2.0, weight)
        else:
            if side == "p":
                lanes = jnp.where(lane == PLACE[BACK[name]], pay[1:2], 0.0)
                here = jnp.broadcast_to(jnp.sum(lanes, axis=1, keepdims=True), lane.shape) > 0.5
            else:
                here = flags[PLACE[name]] > 0
            weight = jnp.where(here, LOGIT * weight, 0.0)
        weight = weight.astype(jnp.bfloat16)
        left[side] -= 1
        total = totals[side]
        out = left[side] == 0 and final[side]
        step = WIDTH // 4 if out else WIDTH
        for start in range(0, WIDTH, step):
            span = slice(start, start + step)
            part = jnp.dot(weight, other[:, span], preferred_element_type=jnp.float32)
            if side in begun:
                total[:, span] += part
            elif earlier[side] is None:
                total[:, span] = part
            else:
                total[:, span] = arrays[earlier[side]][:, span] + part
            if out:
                sem = sems[side].at[start // step]
                copy = pltpu.make_async_copy(total.at[:, span], outs[sides.index(side)].at[:, span], sem)
                copy.start()
                sent.append(copy)
        begun.add(side)
    for copy in sent:
        copy.wait()


def parts(name, common, from_p, steps, earlier, final=()):
    arrays = []

    def at(spot):
        for i, array in enumerate(arrays):
            if array is spot[0]:
                return i, spot[1]
        arrays.append(spot[0])
        return len(arrays) - 1, spot[1]

    plan = [(side, slot, at(block), at(scores)) for side, slot, block, scores in steps]
    sides = sorted(earlier)
    begin = {side: None if earlier[side] is None else at((earlier[side], None))[0] for side in sides}
    scratch = []
    for side in sides:
        scratch += [pltpu.VMEM((BLK, WIDTH), jnp.float32), pltpu.SemaphoreType.DMA((4,))] * (side in final)
    last = {side: side in final for side in sides}
    return pl.pallas_call(
        functools.partial(parts_kernel, plan, begin, last, len(arrays)),
        in_specs=[SMEM] + [VMEM] * (13 + len(arrays)),
        out_specs=[HBM if last[side] else VMEM for side in sides],
        out_shape=[jax.ShapeDtypeStruct((BLK, WIDTH), jnp.float32)] * len(sides),
        scratch_shapes=scratch,
        compiler_params=LIMIT,
        cost_estimate=FREE,
        name=name,
    )(*common, *from_p, *arrays)


def body(queries, passages, positives, pair_blocks, negative_pair_count):
    blocks = lax.axis_size(AXES)
    sign = 1 - 2 * lax.axis_index("cores")
    offsets = jnp.array([SLOTS[name] for name in NAMES], jnp.int32)
    targets = (lax.axis_index(AXES) + sign * offsets) % blocks
    used = jnp.arange(pair_blocks.shape[1], dtype=jnp.int32) < negative_pair_count[0]
    listed = jnp.any((pair_blocks == targets[:, None]) & used[None, :], axis=1)
    flags = (listed | (offsets == 0)).astype(jnp.int32)

    v = dict(flags=flags, pos=positives, q=queries, p=passages)

    def fence():
        keys = sorted(v)
        v.update(zip(keys, lax.optimization_barrier(tuple(v[key] for key in keys))))

    def stat(g):
        v["s%d" % g], v["st%d" % g] = stats_of(
            g, v["flags"], v["pos"], v["q"], [v["p_" + name] for name in GROUPS[g]]
        )

    def group_of(what):
        return [v["%s%d" % (what, g)] for g in range(5)]

    v["p_own"] = v.pop("p")
    v["p_s0"], v["q_s0"] = swap(v["p_own"]), swap(v["q"])
    p_sb = split(v["p_s0"], 1, -1)
    v["p_a"] = split(v["p_own"], 1, -1)
    stat(0)
    fence()
    p_r2, p_sa = split(v["p_a"], 1, -1), swap(v["p_a"])
    v["p_sb"] = p_sb
    fence()
    p_r4, p_b = split(v["p_sb"], 1, -1), swap(v["p_sb"])
    v["q0"] = pair(v["q"], v["q_s0"])
    v["p_r2"], v["p_sa"] = p_r2, p_sa
    fence()
    stat(1)
    q1 = split(after(v["q0"], v["st1"]), 1, -1)
    v["p_b"] = p_b
    stat(2)
    v["p_r4"] = p_r4
    fence()
    v["p_s4"] = swap(v["p_r4"])
    stat(3)
    stat(4)
    line = jax.ShapeDtypeStruct((1, BLK), jnp.float32)
    q_pay, query_loss = call(lse_q_kernel, "lse_q", [small(), line], v["flags"], *group_of("st"), first=SMEM)
    x0, x1, x2, x4 = (swap(v[stats]) for stats in ("st0", "st1", "st2", "st4"))
    near = call(
        near_kernel, "near", small(6), v["st1"], x1, v["st2"], x2, v["st3"], x4, q_pay, swap(q_pay)
    )
    v["one"] = split(near, -1, 1)
    v["two"] = split(v["one"], -1, 1)
    v["one_peer"] = swap(v["one"])
    v["x0"], v["near"], v["q_pay"] = x0, near, q_pay
    v["t0"] = tscores_of(v["p_own"], v["q0"])
    v["q1"] = q1
    fence()
    v["q3"] = split(v["q1"], 1, -1)
    v["q2"] = swap(v["q1"])
    two_peer = swap(v["two"])
    p_pay, passage_loss = call(
        lse_p_kernel, "lse_p", [small(), line], v["st0"], v["x0"], v["one"], v["one_peer"], v["two"], two_peer
    )
    m0 = pair(p_pay, swap(p_pay))

    common = (v["flags"], v["pos"], v["q_pay"], p_pay, v["near"], v["one"], v["one_peer"], v["two"], two_peer)
    places = dict(
        own=("q0", 0), s0=("q0", 1), a=("q1", 0), sb=("q1", 1), sa=("q2", 0), b=("q2", 1), r2=("q3", 0),
        r4=("q3", 1), s4=("q4", 1),
    )

    def steps_of(side, *names):
        steps = []
        for name in names:
            if side == "q":
                g, k = SPOT[name]
                steps.append(("q", name, (v["p_" + name], None), (v["s%d" % g], k)))
            else:
                array, k = places[name]
                scores = (v["t0"], k) if array == "q0" else (v["p_own"], None)
                steps.append(("p", name, (v[array], k), scores))
        return steps

    hold = lax.optimization_barrier
    m1 = split(m0, -1, 1)
    steps = steps_of("q", "own", "s0") + steps_of("p", "own", "s0", "sa", "b")
    p_total, q_total = parts("part0", common, [m0] * 5, steps, dict(p=None, q=None))
    m1, q_total, p_total = hold((m1, q_total, p_total))
    m3 = split(m1, -1, 1)
    m2 = swap(m1)
    steps = steps_of("q", "sa", "b") + steps_of("p", "a", "sb")
    p_total, q_total = parts("part1", common, [m0, m1, m0, m0, m0], steps, dict(p=p_total, q=q_total))
    m2, m3, q_total, p_total = hold((m2, m3, q_total, p_total))
    m4 = swap(m3)
    m4, v["q3"] = hold((m4, v["q3"]))
    v["q4"] = swap(v["q3"])
    messages = [m0, m1, m2, m3, m4]
    (query_grad,) = parts(
        "part2", common, messages, steps_of("q", "a", "sb", "s4", "r4", "r2"), dict(q=q_total), "q"
    )
    v["q4"], p_total, _ = hold((v["q4"], p_total, query_grad))
    (passage_grad,) = parts("part3", common, messages, steps_of("p", "r2", "r4", "s4"), dict(p=p_total), "p")
    return (query_loss, passage_loss, query_grad, passage_grad)


def solution(mesh):
    spec = P(AXES, None)
    return jax.shard_map(
        body,
        mesh=mesh,
        in_specs=(spec, spec, spec, spec, P(AXES)),
        out_specs=(spec, spec, spec, spec),
        check_vma=False,
    )
```

```python
import functools

import jax
import jax.numpy as jnp
from jax import lax
from jax.experimental import pallas as pl
from jax.experimental.pallas import tpu as pltpu
from jax.sharding import PartitionSpec as P

AXES = ("dp", "cores")
LOGIT = 20.0
FAR = -1e30
BLK = 512
WIDTH = 1024
MIB = 1 << 20
SLOTS = dict(own=0, s0=1, a=-2, sa=3, sb=-1, b=2, r2=-4, r4=-3, s4=4)
NAMES = tuple(SLOTS)
GROUPS = (("own", "s0"), ("a", "sa"), ("sb", "b"), ("r2", "r4"), ("s4",))
PLACE = {name: i for i, name in enumerate(NAMES)}
SPOT = {name: (g, i) for g, names in enumerate(GROUPS) for i, name in enumerate(names)}
BACK = dict(own="own", s0="s0", a="b", b="a", r2="s4", s4="r2", sa="sa", sb="sb", r4="r4")
MESSAGE = dict(
    own=(0, 0), s0=(0, 1), b=(1, 0), sa=(1, 1), sb=(2, 0), a=(2, 1), s4=(3, 0), r4=(4, 0), r2=(4, 1)
)

VMEM = pl.BlockSpec(memory_space=pltpu.VMEM)
SMEM = pl.BlockSpec(memory_space=pltpu.SMEM)
HBM = pl.BlockSpec(memory_space=pltpu.HBM)
FREE = pl.CostEstimate(flops=0, bytes_accessed=0, transcendentals=0)
LIMIT = pltpu.CompilerParams(vmem_limit_bytes=16 * MIB)


def split(value, by_core0, by_core1):
    n = lax.axis_size(AXES)
    pairs = [(i, (i + 2 * (by_core1 if i % 2 else by_core0)) % n) for i in range(n)]
    return lax.ppermute(value, AXES, pairs)


def swap(value):
    n = lax.axis_size(AXES)
    return lax.ppermute(value, AXES, [(i, i ^ 1) for i in range(n)])


def after(value, *others):
    return lax.optimization_barrier((value,) + others)[0]


def small(*lead):
    return jax.ShapeDtypeStruct(lead + (8, BLK), jnp.float32)


def call(kernel, name, outs, *operands, first=VMEM):
    return pl.pallas_call(
        kernel,
        in_specs=[first] + [VMEM] * (len(operands) - 1),
        out_specs=jax.tree.map(lambda _: VMEM, outs),
        out_shape=outs,
        compiler_params=LIMIT,
        cost_estimate=FREE,
        name=name,
    )(*operands)


def column_of(row):
    return jnp.transpose(jnp.broadcast_to(row, (128, row.shape[1])))[:, 0:1]


def rows_of(*columns):
    lane = lax.broadcasted_iota(jnp.int32, (columns[0].shape[0], 128), 1)
    packed = jnp.zeros(lane.shape, jnp.float32)
    for i, column in enumerate(columns):
        packed = jnp.where(lane == i, column, packed)
    return jnp.transpose(packed)[0:8]


def scores_of(rows, columns):
    return LOGIT * lax.dot_general(
        rows, columns, (((1,), (1,)), ((), ())), preferred_element_type=jnp.float32
    )


def chosen_of(positives):
    return column_of(positives[...].astype(jnp.float32)).astype(jnp.int32)


def pair_kernel(mine, peer, out):
    out[0] = mine[...]
    out[1] = peer[...]


def pair(mine, peer):
    return call(pair_kernel, "pair", jax.ShapeDtypeStruct((2,) + mine.shape, mine.dtype), mine, peer)


def stats_kernel(names, flags, positives, queries, *refs):
    passages, (scores, stats) = refs[:-2], refs[-2:]
    for i, name in enumerate(names):
        s = scores_of(queries[...], passages[i][...])
        scores[i] = s
        row_top = jnp.max(s, axis=1, keepdims=True)
        row_total = jnp.sum(jnp.exp(s - row_top), axis=1, keepdims=True)
        col_top = jnp.max(s, axis=0, keepdims=True)
        col_total = jnp.sum(jnp.exp(s - col_top), axis=0, keepdims=True)
        if name == "own":
            hit = jnp.where(lax.broadcasted_iota(jnp.int32, s.shape, 1) == chosen_of(positives), s, 0.0)
            packed = rows_of(row_top, row_total, jnp.sum(hit, axis=1, keepdims=True))
            stats[i, 0:2] = packed[0:2]
            stats[i, 2:3] = col_top
            stats[i, 3:4] = col_total
            stats[i, 4:5] = packed[2:3]
            stats[i, 5:6] = jnp.sum(hit, axis=0, keepdims=True)
        else:
            here = flags[PLACE[name]] > 0
            packed = rows_of(row_top, row_total)
            stats[i, 0:1] = jnp.where(here, packed[0:1], FAR)
            stats[i, 1:2] = jnp.where(here, packed[1:2], 0.0)
            stats[i, 2:3] = jnp.where(here, col_top, FAR)
            stats[i, 3:4] = jnp.where(here, col_total, 0.0)


def stats_of(g, flags, positives, queries, passages):
    n = len(GROUPS[g])
    outs = [jax.ShapeDtypeStruct((n, BLK, BLK), jnp.float32), small(n)]
    kernel = functools.partial(stats_kernel, GROUPS[g])
    return call(kernel, "stats%d" % g, outs, flags, positives, queries, *passages, first=SMEM)


def merged(parts, at):
    tops, totals = [p[at : at + 1] for p in parts], [p[at + 1 : at + 2] for p in parts]
    top = functools.reduce(jnp.maximum, tops)
    return top, sum(total * jnp.exp(t - top) for t, total in zip(tops, totals))


def merge_into(out, *parts):
    out[2:3], out[3:4] = merged(parts, 2)


def lse_q_kernel(flags, *refs):
    stats, (pay, loss) = refs[:5], refs[5:]
    top, total = merged([stats[SPOT[name][0]].at[SPOT[name][1]] for name in NAMES], 0)
    lse = top + jnp.log(total)
    lane = lax.broadcasted_iota(jnp.int32, (1, BLK), 1)
    here = jnp.zeros((1, BLK), jnp.float32)
    for i in range(9):
        here = jnp.where(lane == i, flags[i].astype(jnp.float32), here)
    pay[0:1] = lse
    pay[1:2] = here
    loss[...] = lse - stats[0][0, 4:5]


def near_kernel(st1, peer1, st2, peer2, st3, peer4, pay, peer_pay, out):
    merge_into(out.at[0], st1.at[0], peer1.at[1])
    merge_into(out.at[1], st2.at[0], peer2.at[1])
    out[2] = st3[0]
    merge_into(out.at[3], st3.at[1], peer4.at[0])
    out[4] = pay[...]
    out[5] = peer_pay[...]


def lse_p_kernel(st0, peer0, one, one_peer, two, two_peer, pay, loss):
    parts = [st0.at[0], peer0.at[1], one.at[0], one_peer.at[1], two.at[2], two_peer.at[3]]
    top, total = merged(parts, 2)
    lse = top + jnp.log(total)
    pay[0:1] = lse
    loss[...] = lse - st0[0, 5:6]


def tscores_kernel(passages, queries, out):
    for i in range(out.shape[0]):
        out[i] = scores_of(passages[...], queries[i])


def tscores_of(passages, queries):
    out = jax.ShapeDtypeStruct((queries.shape[0], BLK, BLK), jnp.float32)
    return call(tscores_kernel, "tscores", out, passages, queries)


def parts_kernel(steps, earlier, final, n_arrays, *refs):
    flags, positives, own_rows, own_columns, refs = *refs[:4], refs[4:]
    from_q, from_p, refs = refs[:5], refs[5:10], refs[10:]
    arrays, refs = refs[:n_arrays], refs[n_arrays:]
    sides = sorted(earlier)
    outs, scratch = refs[: len(sides)], refs[len(sides) :]
    totals, sems = {}, {}
    for side, out in zip(sides, outs):
        if final[side]:
            totals[side], sems[side], *scratch = scratch
        else:
            totals[side] = out
    lane = lax.broadcasted_iota(jnp.int32, (1, BLK), 1)
    own_lse = {side: column_of((own_rows if side == "q" else own_columns)[0:1]) for side in sides}
    left = {side: sum(step[0] == side for step in steps) for side in sides}
    begun = set()
    sent = []
    for side, name, block, score in steps:
        message, which = MESSAGE[name]
        pay = from_q[message].at[4 + which] if side == "p" else from_p[message].at[which]
        other = arrays[block[0]] if block[1] is None else arrays[block[0]].at[block[1]]
        if score[1] is None:
            s = scores_of(arrays[score[0]][...], other[...])
        else:
            s = arrays[score[0]][score[1]]
        weight = jnp.exp(s - own_lse[side]) + jnp.exp(s - pay[0:1])
        if name == "own":
            if side == "p":
                hit = lax.broadcasted_iota(jnp.int32, s.shape, 0) == positives[...]
            else:
                hit = lax.broadcasted_iota(jnp.int32, s.shape, 1) == chosen_of(positives)
            weight = LOGIT * jnp.where(hit, weight - 2.0, weight)
        else:
            if side == "p":
                lanes = jnp.where(lane == PLACE[BACK[name]], pay[1:2], 0.0)
                here = jnp.broadcast_to(jnp.sum(lanes, axis=1, keepdims=True), lane.shape) > 0.5
            else:
                here = flags[PLACE[name]] > 0
            weight = jnp.where(here, LOGIT * weight, 0.0)
        weight = weight.astype(jnp.bfloat16)
        left[side] -= 1
        total = totals[side]
        out = left[side] == 0 and final[side]
        step = WIDTH // 4 if out else WIDTH
        for start in range(0, WIDTH, step):
            span = slice(start, start + step)
            part = jnp.dot(weight, other[:, span], preferred_element_type=jnp.float32)
            if side in begun:
                total[:, span] += part
            elif earlier[side] is None:
                total[:, span] = part
            else:
                total[:, span] = arrays[earlier[side]][:, span] + part
            if out:
                sem = sems[side].at[start // step]
                copy = pltpu.make_async_copy(total.at[:, span], outs[sides.index(side)].at[:, span], sem)
                copy.start()
                sent.append(copy)
        begun.add(side)
    for copy in sent:
        copy.wait()


def parts(name, common, from_p, steps, earlier, final=()):
    arrays = []

    def at(spot):
        for i, array in enumerate(arrays):
            if array is spot[0]:
                return i, spot[1]
        arrays.append(spot[0])
        return len(arrays) - 1, spot[1]

    plan = [(side, slot, at(block), at(scores)) for side, slot, block, scores in steps]
    sides = sorted(earlier)
    begin = {side: None if earlier[side] is None else at((earlier[side], None))[0] for side in sides}
    scratch = []
    for side in sides:
        scratch += [pltpu.VMEM((BLK, WIDTH), jnp.float32), pltpu.SemaphoreType.DMA((4,))] * (side in final)
    last = {side: side in final for side in sides}
    return pl.pallas_call(
        functools.partial(parts_kernel, plan, begin, last, len(arrays)),
        in_specs=[SMEM] + [VMEM] * (13 + len(arrays)),
        out_specs=[HBM if last[side] else VMEM for side in sides],
        out_shape=[jax.ShapeDtypeStruct((BLK, WIDTH), jnp.float32)] * len(sides),
        scratch_shapes=scratch,
        compiler_params=LIMIT,
        cost_estimate=FREE,
        name=name,
    )(*common, *from_p, *arrays)


def body(queries, passages, positives, pair_blocks, negative_pair_count):
    blocks = lax.axis_size(AXES)
    sign = 1 - 2 * lax.axis_index("cores")
    offsets = jnp.array([SLOTS[name] for name in NAMES], jnp.int32)
    targets = (lax.axis_index(AXES) + sign * offsets) % blocks
    used = jnp.arange(pair_blocks.shape[1], dtype=jnp.int32) < negative_pair_count[0]
    listed = jnp.any((pair_blocks == targets[:, None]) & used[None, :], axis=1)
    flags = (listed | (offsets == 0)).astype(jnp.int32)

    v = dict(flags=flags, pos=positives, q=queries, p=passages)

    def fence():
        keys = sorted(v)
        v.update(zip(keys, lax.optimization_barrier(tuple(v[key] for key in keys))))

    def stat(g):
        v["s%d" % g], v["st%d" % g] = stats_of(
            g, v["flags"], v["pos"], v["q"], [v["p_" + name] for name in GROUPS[g]]
        )

    def group_of(what):
        return [v["%s%d" % (what, g)] for g in range(5)]

    v["p_own"] = v.pop("p")
    v["p_s0"], v["q_s0"] = swap(v["p_own"]), swap(v["q"])
    p_sb = split(v["p_s0"], 1, -1)
    v["p_a"] = split(v["p_own"], 1, -1)
    stat(0)
    fence()
    p_r2, p_sa = split(v["p_a"], 1, -1), swap(v["p_a"])
    v["p_sb"] = p_sb
    fence()
    p_r4, p_b = split(v["p_sb"], 1, -1), swap(v["p_sb"])
    v["q0"] = pair(v["q"], v["q_s0"])
    v["p_r2"], v["p_sa"] = p_r2, p_sa
    fence()
    stat(1)
    q1 = split(after(v["q0"], v["st1"]), 1, -1)
    v["p_b"] = p_b
    stat(2)
    v["p_r4"] = p_r4
    fence()
    v["p_s4"] = swap(v["p_r4"])
    stat(3)
    stat(4)
    line = jax.ShapeDtypeStruct((1, BLK), jnp.float32)
    q_pay, query_loss = call(lse_q_kernel, "lse_q", [small(), line], v["flags"], *group_of("st"), first=SMEM)
    x0, x1, x2, x4 = (swap(v[stats]) for stats in ("st0", "st1", "st2", "st4"))
    near = call(
        near_kernel, "near", small(6), v["st1"], x1, v["st2"], x2, v["st3"], x4, q_pay, swap(q_pay)
    )
    v["one"] = split(near, -1, 1)
    v["two"] = split(near, -2, 2)
    v["one_peer"] = swap(v["one"])
    v["x0"], v["near"], v["q_pay"] = x0, near, q_pay
    v["t0"] = tscores_of(v["p_own"], v["q0"])
    v["q1"] = q1
    fence()
    v["q3"] = split(v["q1"], 1, -1)
    v["q2"] = swap(v["q1"])
    two_peer = swap(v["two"])
    p_pay, passage_loss = call(
        lse_p_kernel, "lse_p", [small(), line], v["st0"], v["x0"], v["one"], v["one_peer"], v["two"], two_peer
    )
    m0 = pair(p_pay, swap(p_pay))

    common = (v["flags"], v["pos"], v["q_pay"], p_pay, v["near"], v["one"], v["one_peer"], v["two"], two_peer)
    places = dict(
        own=("q0", 0), s0=("q0", 1), a=("q1", 0), sb=("q1", 1), sa=("q2", 0), b=("q2", 1), r2=("q3", 0),
        r4=("q3", 1), s4=("q4", 1),
    )

    def steps_of(side, *names):
        steps = []
        for name in names:
            if side == "q":
                g, k = SPOT[name]
                steps.append(("q", name, (v["p_" + name], None), (v["s%d" % g], k)))
            else:
                array, k = places[name]
                scores = (v["t0"], k) if array == "q0" else (v["p_own"], None)
                steps.append(("p", name, (v[array], k), scores))
        return steps

    hold = lax.optimization_barrier
    m1 = split(m0, -1, 1)
    steps = steps_of("q", "own", "s0") + steps_of("p", "own", "s0", "sa", "b")
    p_total, q_total = parts("part0", common, [m0] * 5, steps, dict(p=None, q=None))
    m1, q_total, p_total = hold((m1, q_total, p_total))
    m3 = split(m1, -1, 1)
    m2 = swap(m1)
    steps = steps_of("q", "sa", "b") + steps_of("p", "a", "sb")
    p_total, q_total = parts("part1", common, [m0, m1, m0, m0, m0], steps, dict(p=p_total, q=q_total))
    m2, m3, q_total, p_total = hold((m2, m3, q_total, p_total))
    m4 = swap(m3)
    m4, v["q3"] = hold((m4, v["q3"]))
    v["q4"] = swap(v["q3"])
    messages = [m0, m1, m2, m3, m4]
    steps = steps_of("p", "r2", "r4") + steps_of("q", "a", "sb", "s4", "r4", "r2")
    p_total, query_grad = parts("part2", common, messages, steps, dict(p=p_total, q=q_total), "q")
    v["q4"], p_total, _ = hold((v["q4"], p_total, query_grad))
    (passage_grad,) = parts("part3", common, messages, steps_of("p", "s4"), dict(p=p_total), "p")
    return (query_loss, passage_loss, query_grad, passage_grad)


def solution(mesh):
    spec = P(AXES, None)
    return jax.shard_map(
        body,
        mesh=mesh,
        in_specs=(spec, spec, spec, spec, P(AXES)),
        out_specs=(spec, spec, spec, spec),
        check_vma=False,
    )
```

```python
import functools

import jax
import jax.numpy as jnp
from jax import lax
from jax.experimental import pallas as pl
from jax.experimental.pallas import tpu as pltpu
from jax.sharding import PartitionSpec as P

AXES = ("dp", "cores")
LOGIT = 20.0
FAR = -1e30
BLK = 512
WIDTH = 1024
MIB = 1 << 20
SLOTS = dict(own=0, s0=1, a=-2, sa=3, sb=-1, b=2, r2=-4, r4=-3, s4=4)
NAMES = tuple(SLOTS)
GROUPS = (("own", "s0"), ("a", "sa"), ("sb", "b"), ("r2", "r4"), ("s4",))
PLACE = {name: i for i, name in enumerate(NAMES)}
SPOT = {name: (g, i) for g, names in enumerate(GROUPS) for i, name in enumerate(names)}
BACK = dict(own="own", s0="s0", a="b", b="a", r2="s4", s4="r2", sa="sa", sb="sb", r4="r4")
MESSAGE = dict(
    own=(0, 0), s0=(0, 1), b=(1, 0), sa=(1, 1), sb=(2, 0), a=(2, 1), s4=(3, 0), r4=(4, 0), r2=(4, 1)
)

VMEM = pl.BlockSpec(memory_space=pltpu.VMEM)
SMEM = pl.BlockSpec(memory_space=pltpu.SMEM)
HBM = pl.BlockSpec(memory_space=pltpu.HBM)
FREE = pl.CostEstimate(flops=0, bytes_accessed=0, transcendentals=0)
LIMIT = pltpu.CompilerParams(vmem_limit_bytes=16 * MIB)


def split(value, by_core0, by_core1):
    n = lax.axis_size(AXES)
    pairs = [(i, (i + 2 * (by_core1 if i % 2 else by_core0)) % n) for i in range(n)]
    return lax.ppermute(value, AXES, pairs)


def swap(value):
    n = lax.axis_size(AXES)
    return lax.ppermute(value, AXES, [(i, i ^ 1) for i in range(n)])


def after(value, *others):
    return lax.optimization_barrier((value,) + others)[0]


def small(*lead):
    return jax.ShapeDtypeStruct(lead + (8, BLK), jnp.float32)


def call(kernel, name, outs, *operands, first=VMEM):
    return pl.pallas_call(
        kernel,
        in_specs=[first] + [VMEM] * (len(operands) - 1),
        out_specs=jax.tree.map(lambda _: VMEM, outs),
        out_shape=outs,
        compiler_params=LIMIT,
        cost_estimate=FREE,
        name=name,
    )(*operands)


def column_of(row):
    return jnp.transpose(jnp.broadcast_to(row, (128, row.shape[1])))[:, 0:1]


def rows_of(*columns):
    lane = lax.broadcasted_iota(jnp.int32, (columns[0].shape[0], 128), 1)
    packed = jnp.zeros(lane.shape, jnp.float32)
    for i, column in enumerate(columns):
        packed = jnp.where(lane == i, column, packed)
    return jnp.transpose(packed)[0:8]


def scores_of(rows, columns):
    return LOGIT * lax.dot_general(
        rows, columns, (((1,), (1,)), ((), ())), preferred_element_type=jnp.float32
    )


def chosen_of(positives):
    return column_of(positives[...].astype(jnp.float32)).astype(jnp.int32)


def pair_kernel(mine, peer, out):
    out[0] = mine[...]
    out[1] = peer[...]


def pair(mine, peer):
    return call(pair_kernel, "pair", jax.ShapeDtypeStruct((2,) + mine.shape, mine.dtype), mine, peer)


def stats_kernel(names, flags, positives, queries, *refs):
    passages, (scores, stats) = refs[:-2], refs[-2:]
    for i, name in enumerate(names):
        s = scores_of(queries[...], passages[i][...])
        scores[i] = s
        row_top = jnp.max(s, axis=1, keepdims=True)
        row_total = jnp.sum(jnp.exp(s - row_top), axis=1, keepdims=True)
        col_top = jnp.max(s, axis=0, keepdims=True)
        col_total = jnp.sum(jnp.exp(s - col_top), axis=0, keepdims=True)
        if name == "own":
            hit = jnp.where(lax.broadcasted_iota(jnp.int32, s.shape, 1) == chosen_of(positives), s, 0.0)
            packed = rows_of(row_top, row_total, jnp.sum(hit, axis=1, keepdims=True))
            stats[i, 0:2] = packed[0:2]
            stats[i, 2:3] = col_top
            stats[i, 3:4] = col_total
            stats[i, 4:5] = packed[2:3]
            stats[i, 5:6] = jnp.sum(hit, axis=0, keepdims=True)
        else:
            here = flags[PLACE[name]] > 0
            packed = rows_of(row_top, row_total)
            stats[i, 0:1] = jnp.where(here, packed[0:1], FAR)
            stats[i, 1:2] = jnp.where(here, packed[1:2], 0.0)
            stats[i, 2:3] = jnp.where(here, col_top, FAR)
            stats[i, 3:4] = jnp.where(here, col_total, 0.0)


def stats_of(g, flags, positives, queries, passages):
    n = len(GROUPS[g])
    outs = [jax.ShapeDtypeStruct((n, BLK, BLK), jnp.float32), small(n)]
    kernel = functools.partial(stats_kernel, GROUPS[g])
    return call(kernel, "stats%d" % g, outs, flags, positives, queries, *passages, first=SMEM)


def merged(parts, at):
    tops, totals = [p[at : at + 1] for p in parts], [p[at + 1 : at + 2] for p in parts]
    top = functools.reduce(jnp.maximum, tops)
    return top, sum(total * jnp.exp(t - top) for t, total in zip(tops, totals))


def merge_into(out, *parts):
    out[2:3], out[3:4] = merged(parts, 2)


def lse_q_kernel(flags, *refs):
    stats, (pay, loss) = refs[:5], refs[5:]
    top, total = merged([stats[SPOT[name][0]].at[SPOT[name][1]] for name in NAMES], 0)
    lse = top + jnp.log(total)
    lane = lax.broadcasted_iota(jnp.int32, (1, BLK), 1)
    here = jnp.zeros((1, BLK), jnp.float32)
    for i in range(9):
        here = jnp.where(lane == i, flags[i].astype(jnp.float32), here)
    pay[0:1] = lse
    pay[1:2] = here
    loss[...] = lse - stats[0][0, 4:5]


def near_kernel(st1, peer1, st2, peer2, st3, peer4, pay, peer_pay, out):
    merge_into(out.at[0], st1.at[0], peer1.at[1])
    merge_into(out.at[1], st2.at[0], peer2.at[1])
    out[2] = st3[0]
    merge_into(out.at[3], st3.at[1], peer4.at[0])
    out[4] = pay[...]
    out[5] = peer_pay[...]


def lse_p_kernel(st0, peer0, one, one_peer, two, two_peer, pay, loss):
    parts = [st0.at[0], peer0.at[1], one.at[0], one_peer.at[1], two.at[2], two_peer.at[3]]
    top, total = merged(parts, 2)
    lse = top + jnp.log(total)
    pay[0:1] = lse
    loss[...] = lse - st0[0, 5:6]


def tscores_kernel(passages, queries, out):
    for i in range(out.shape[0]):
        out[i] = scores_of(passages[...], queries[i])


def tscores_of(passages, queries):
    out = jax.ShapeDtypeStruct((queries.shape[0], BLK, BLK), jnp.float32)
    return call(tscores_kernel, "tscores", out, passages, queries)


def parts_kernel(steps, earlier, final, n_arrays, *refs):
    flags, positives, own_rows, own_columns, refs = *refs[:4], refs[4:]
    from_q, from_p, refs = refs[:5], refs[5:10], refs[10:]
    arrays, refs = refs[:n_arrays], refs[n_arrays:]
    sides = sorted(earlier)
    outs, scratch = refs[: len(sides)], refs[len(sides) :]
    totals, sems = {}, {}
    for side, out in zip(sides, outs):
        if final[side]:
            totals[side], sems[side], *scratch = scratch
        else:
            totals[side] = out
    lane = lax.broadcasted_iota(jnp.int32, (1, BLK), 1)
    own_lse = {side: column_of((own_rows if side == "q" else own_columns)[0:1]) for side in sides}
    left = {side: sum(step[0] == side for step in steps) for side in sides}
    begun = set()
    sent = []
    for side, name, block, score in steps:
        message, which = MESSAGE[name]
        pay = from_q[message].at[4 + which] if side == "p" else from_p[message].at[which]
        other = arrays[block[0]] if block[1] is None else arrays[block[0]].at[block[1]]
        if score[1] is None:
            s = scores_of(arrays[score[0]][...], other[...])
        else:
            s = arrays[score[0]][score[1]]
        weight = jnp.exp(s - own_lse[side]) + jnp.exp(s - pay[0:1])
        if name == "own":
            if side == "p":
                hit = lax.broadcasted_iota(jnp.int32, s.shape, 0) == positives[...]
            else:
                hit = lax.broadcasted_iota(jnp.int32, s.shape, 1) == chosen_of(positives)
            weight = LOGIT * jnp.where(hit, weight - 2.0, weight)
        else:
            if side == "p":
                lanes = jnp.where(lane == PLACE[BACK[name]], pay[1:2], 0.0)
                here = jnp.broadcast_to(jnp.sum(lanes, axis=1, keepdims=True), lane.shape) > 0.5
            else:
                here = flags[PLACE[name]] > 0
            weight = jnp.where(here, LOGIT * weight, 0.0)
        weight = weight.astype(jnp.bfloat16)
        left[side] -= 1
        total = totals[side]
        out = left[side] == 0 and final[side]
        step = WIDTH // 4 if out else WIDTH
        for start in range(0, WIDTH, step):
            span = slice(start, start + step)
            part = jnp.dot(weight, other[:, span], preferred_element_type=jnp.float32)
            if side in begun:
                total[:, span] += part
            elif earlier[side] is None:
                total[:, span] = part
            else:
                total[:, span] = arrays[earlier[side]][:, span] + part
            if out:
                sem = sems[side].at[start // step]
                copy = pltpu.make_async_copy(total.at[:, span], outs[sides.index(side)].at[:, span], sem)
                copy.start()
                sent.append(copy)
        begun.add(side)
    for copy in sent:
        copy.wait()


def parts(name, common, from_p, steps, earlier, final=()):
    arrays = []

    def at(spot):
        for i, array in enumerate(arrays):
            if array is spot[0]:
                return i, spot[1]
        arrays.append(spot[0])
        return len(arrays) - 1, spot[1]

    plan = [(side, slot, at(block), at(scores)) for side, slot, block, scores in steps]
    sides = sorted(earlier)
    begin = {side: None if earlier[side] is None else at((earlier[side], None))[0] for side in sides}
    scratch = []
    for side in sides:
        scratch += [pltpu.VMEM((BLK, WIDTH), jnp.float32), pltpu.SemaphoreType.DMA((4,))] * (side in final)
    last = {side: side in final for side in sides}
    return pl.pallas_call(
        functools.partial(parts_kernel, plan, begin, last, len(arrays)),
        in_specs=[SMEM] + [VMEM] * (13 + len(arrays)),
        out_specs=[HBM if last[side] else VMEM for side in sides],
        out_shape=[jax.ShapeDtypeStruct((BLK, WIDTH), jnp.float32)] * len(sides),
        scratch_shapes=scratch,
        compiler_params=LIMIT,
        cost_estimate=FREE,
        name=name,
    )(*common, *from_p, *arrays)


def body(queries, passages, positives, pair_blocks, negative_pair_count):
    blocks = lax.axis_size(AXES)
    sign = 1 - 2 * lax.axis_index("cores")
    offsets = jnp.array([SLOTS[name] for name in NAMES], jnp.int32)
    targets = (lax.axis_index(AXES) + sign * offsets) % blocks
    used = jnp.arange(pair_blocks.shape[1], dtype=jnp.int32) < negative_pair_count[0]
    listed = jnp.any((pair_blocks == targets[:, None]) & used[None, :], axis=1)
    flags = (listed | (offsets == 0)).astype(jnp.int32)

    v = dict(flags=flags, pos=positives, q=queries, p=passages)

    def fence():
        keys = sorted(v)
        v.update(zip(keys, lax.optimization_barrier(tuple(v[key] for key in keys))))

    def stat(g):
        v["s%d" % g], v["st%d" % g] = stats_of(
            g, v["flags"], v["pos"], v["q"], [v["p_" + name] for name in GROUPS[g]]
        )

    def group_of(what):
        return [v["%s%d" % (what, g)] for g in range(5)]

    v["p_own"] = v.pop("p")
    v["p_s0"], v["q_s0"] = swap(v["p_own"]), swap(v["q"])
    p_sb = split(v["p_s0"], 1, -1)
    v["p_a"] = split(v["p_own"], 1, -1)
    stat(0)
    fence()
    p_r2, p_sa = split(v["p_a"], 1, -1), swap(v["p_a"])
    v["p_sb"] = p_sb
    fence()
    p_r4, p_b = split(v["p_sb"], 1, -1), swap(v["p_sb"])
    v["q0"] = pair(v["q"], v["q_s0"])
    v["p_r2"], v["p_sa"] = p_r2, p_sa
    fence()
    stat(1)
    q1 = split(after(v["q0"], v["st1"]), 1, -1)
    v["p_b"] = p_b
    stat(2)
    v["p_r4"] = p_r4
    fence()
    v["p_s4"] = swap(v["p_r4"])
    stat(3)
    stat(4)
    line = jax.ShapeDtypeStruct((1, BLK), jnp.float32)
    q_pay, query_loss = call(lse_q_kernel, "lse_q", [small(), line], v["flags"], *group_of("st"), first=SMEM)
    x0, x1, x2, x4 = (swap(v[stats]) for stats in ("st0", "st1", "st2", "st4"))
    near = call(
        near_kernel, "near", small(6), v["st1"], x1, v["st2"], x2, v["st3"], x4, q_pay, swap(q_pay)
    )
    v["one"] = split(near, -1, 1)
    v["two"] = split(near, -2, 2)
    v["one_peer"] = swap(v["one"])
    v["x0"], v["near"], v["q_pay"] = x0, near, q_pay
    v["t0"] = tscores_of(v["p_own"], v["q0"])
    q3 = split(after(q1, v["one"]), 1, -1)
    fence()
    v["q1"], v["q3"] = after(q1, v["two"]), q3
    v["q2"] = swap(v["q1"])
    two_peer = swap(v["two"])
    p_pay, passage_loss = call(
        lse_p_kernel, "lse_p", [small(), line], v["st0"], v["x0"], v["one"], v["one_peer"], v["two"], two_peer
    )
    m0 = pair(p_pay, swap(p_pay))

    common = (v["flags"], v["pos"], v["q_pay"], p_pay, v["near"], v["one"], v["one_peer"], v["two"], two_peer)
    places = dict(
        own=("q0", 0), s0=("q0", 1), a=("q1", 0), sb=("q1", 1), sa=("q2", 0), b=("q2", 1), r2=("q3", 0),
        r4=("q3", 1), s4=("q4", 1),
    )

    def steps_of(side, *names):
        steps = []
        for name in names:
            if side == "q":
                g, k = SPOT[name]
                steps.append(("q", name, (v["p_" + name], None), (v["s%d" % g], k)))
            else:
                array, k = places[name]
                scores = (v["t0"], k) if array == "q0" else (v["p_own"], None)
                steps.append(("p", name, (v[array], k), scores))
        return steps

    hold = lax.optimization_barrier
    m1 = split(m0, -1, 1)
    steps = steps_of("q", "own", "s0") + steps_of("p", "own", "s0", "a", "sb")
    p_total, q_total = parts("part0", common, [m0] * 5, steps, dict(p=None, q=None))
    m1, q_total, p_total = hold((m1, q_total, p_total))
    m3 = split(m1, -1, 1)
    m2 = swap(m1)
    steps = steps_of("q", "sa", "b") + steps_of("p", "sa", "b")
    p_total, q_total = parts("part1", common, [m0, m1, m0, m0, m0], steps, dict(p=p_total, q=q_total))
    m2, m3, q_total, p_total = hold((m2, m3, q_total, p_total))
    m4 = swap(m3)
    m4, v["q3"] = hold((m4, v["q3"]))
    v["q4"] = swap(v["q3"])
    messages = [m0, m1, m2, m3, m4]
    steps = steps_of("p", "r2", "r4") + steps_of("q", "a", "sb", "s4", "r4", "r2")
    p_total, query_grad = parts("part2", common, messages, steps, dict(p=p_total, q=q_total), "q")
    v["q4"], p_total, _ = hold((v["q4"], p_total, query_grad))
    (passage_grad,) = parts("part3", common, messages, steps_of("p", "s4"), dict(p=p_total), "p")
    return (query_loss, passage_loss, query_grad, passage_grad)


def solution(mesh):
    spec = P(AXES, None)
    return jax.shard_map(
        body,
        mesh=mesh,
        in_specs=(spec, spec, spec, spec, P(AXES)),
        out_specs=(spec, spec, spec, spec),
        check_vma=False,
    )
```
